512 devices in a mesh: slab: 128 (over z, x, core), col: 4 (over y).
Axes of the slice: x: 4, y: 4, z: 16, core: 2. Of those that a mesh axis runs over, the one named last changes fastest.
Arguments:
- basis: bfloat16 [3, 64, 256, 32, 128], P(None, None, 'slab', 'col')
- cell_map: int32 [256, 32, 128], P('slab', 'col'), may hold values from 0 to 7
- table: float32 [8, 27], replicated, may hold values from 0 to 1, as said below
Outputs:
- next_block: bfloat16 [64, 256, 32, 128], P(None, 'slab', 'col')
- projections: float32 [2, 192, 64], replicated
- triangles: float32 [2, 64, 64], replicated
The draws below stay inside these ranges and needn't reach their ends.
Inputs may be any that keep to these rules, and one draw needn't show every extreme that they name: `table`: coefficients lie between 0 and 1; the centre one is the largest.
All inputs are finite; a program needn't handle non-finite values.
Results may differ from the reference program's by a relative error of at most 0.027.
Values may be sent and summed in bfloat16 or wider, within the bound.
A program may use at most 64 MiB of HBM per device.

```python
import jax
import jax.numpy as jnp
from jax import lax

COLS = 64
BLOCKS = 3
CLASSES = 8
NX = 256
NY = 32
NZ = 128


def draw_table(key, part):
    key = jax.random.fold_in(key, 7)
    offsets = jnp.arange(27)
    dist = jnp.abs(offsets // 9 - 1) + jnp.abs(offsets // 3 % 3 - 1) + jnp.abs(offsets % 3 - 1)
    low = jnp.array([0.6, 0.05, 0.0, 0.0], jnp.float32)[dist]
    high = jnp.array([1.0, 0.25, 0.08, 0.03], jnp.float32)[dist]
    unit = jax.random.uniform(key, (CLASSES, 27), jnp.float32)
    return (low + (high - low) * unit).astype(jnp.float32)


def draw_basis(key, part):
    key = jax.random.fold_in(key, 11)
    key_codes, key_angles, key_signs = jax.random.split(key, 3)
    plane_cells = NX * NY
    columns_all = BLOCKS * COLS
    walsh_codes = (jax.random.permutation(key_codes, plane_cells - 1)[:columns_all] + 1).astype(jnp.int32)
    places = jnp.arange(plane_cells, dtype=jnp.int32)
    masked = walsh_codes[:, None] & places[None, :]
    parity = jnp.zeros((columns_all, plane_cells), jnp.int32)
    for bit in range(plane_cells.bit_length()):
        parity = parity ^ masked >> bit & 1
    rotated = (1.0 - 2.0 * parity.astype(jnp.float32)).reshape(BLOCKS, COLS, plane_cells)
    column_ids = jnp.arange(COLS, dtype=jnp.int32)
    level = 0
    while 1 << level < COLS:
        partner = column_ids ^ 1 << level
        lower_index = jnp.minimum(column_ids, partner)
        angles = jax.random.uniform(jax.random.fold_in(key_angles, level), (BLOCKS, COLS), jnp.float32, -3.14159265, 3.14159265)
        cosine = jnp.cos(angles[:, lower_index])
        sine = jnp.sin(angles[:, lower_index])
        factor = jnp.where((column_ids == lower_index)[None, :], -sine, sine)
        rotated = cosine[:, :, None] * rotated + factor[:, :, None] * rotated[:, partner]
        level = level + 1
    cell_signs = jnp.where(jax.random.bernoulli(key_signs, 0.5, (NX, NY, NZ)), 1.0, -1.0).astype(jnp.float32)
    orthogonal = rotated.reshape(BLOCKS, COLS, NX, NY, 1) * cell_signs[None, None]
    earlier = jnp.concatenate([jnp.zeros_like(orthogonal[:1]), orthogonal[:-1]], axis=0)
    return (orthogonal + 0.4 * earlier).astype(jnp.float32).astype(jnp.bfloat16)


def with_ends(values, rng, least, top_value):
    index_at = [jax.random.randint(jax.random.fold_in(rng, axis), (), 0, length) for axis, length in enumerate(values.shape)]
    main_axis = values.shape.index(max(values.shape))
    next_to = index_at[:main_axis] + [(index_at[main_axis] + 1) % values.shape[main_axis]] + index_at[main_axis + 1:]
    return values.at[tuple(index_at)].set(least).at[tuple(next_to)].set(top_value)


def setup_inputs(seed: int = 0) -> dict:
    seeds = jax.random.split(jax.random.key(seed), 4)
    return {
        "basis": draw_basis(jax.random.fold_in(seeds[3], 71), 0),
        "cell_map": with_ends(jax.random.randint(seeds[1], (NX, NY, NZ), 0, CLASSES), jax.random.fold_in(seeds[1], 1), 0, CLASSES - 1).astype(jnp.int32),
        "table": draw_table(jax.random.fold_in(seeds[3], 71), 0),
    }


def apply_stencil(block, coef):

    def one_column(field):
        padded = jnp.pad(field.astype(jnp.float32), 1)
        nx, ny, nz = field.shape
        total = jnp.zeros((nx, ny, nz), jnp.float32)
        for dx in range(3):
            for dy in range(3):
                for dz in range(3):
                    offset = 9 * dx + 3 * dy + dz
                    total = total + coef[offset] * padded[dx:dx + nx, dy:dy + ny, dz:dz + nz]
        return total.astype(jnp.bfloat16)
    return lax.map(one_column, block)

def gram_of(left, right, scale):
    return lax.dot_general(left.astype(jnp.float32), right.astype(jnp.float32), (((1,), (1,)), ((), ())), preferred_element_type=jnp.float32) * scale

def correct(stack, block, coeffs):
    moved = lax.dot_general(coeffs.astype(jnp.bfloat16).astype(jnp.float32), stack.astype(jnp.float32), (((0,), (0,)), ((), ())), preferred_element_type=jnp.float32)
    return (block.astype(jnp.float32) - moved).astype(jnp.bfloat16)

def orthonormalize(stack, block, scale):
    first = gram_of(stack, block, scale)
    block_one = correct(stack, block, first)
    second = gram_of(stack, block_one, scale)
    block_two = correct(stack, block_one, second)
    square = gram_of(block_two, block_two, scale)
    lower = jnp.linalg.cholesky(square)
    identity = jnp.eye(lower.shape[0], dtype=lower.dtype)
    inverse = lax.linalg.triangular_solve(lower, identity, left_side=True, lower=True)
    result = jnp.dot(inverse.astype(jnp.bfloat16).astype(jnp.float32), block_two.astype(jnp.float32), preferred_element_type=jnp.float32).astype(jnp.bfloat16)
    return (result, first + second, lower)

def reference(basis, cell_map, table):
    coef = jnp.moveaxis(table[cell_map], -1, 0)
    cells = NX * NY * NZ
    scale = 1.0 / cells
    flat = basis.reshape(BLOCKS * COLS, cells)
    image = apply_stencil(basis[2], coef).reshape(COLS, cells)
    block_one, proj_one, lower_one = orthonormalize(flat, image, scale)
    stack = jnp.concatenate([flat[COLS:], block_one], axis=0)
    image = apply_stencil(block_one.reshape(COLS, NX, NY, NZ), coef).reshape(COLS, cells)
    block_two, proj_two, lower_two = orthonormalize(stack, image, scale)
    return (block_two.reshape(COLS, NX, NY, NZ), jnp.stack([proj_one, proj_two]), jnp.stack([lower_one, lower_two]))
```

```python
import functools

import jax
import jax.numpy as jnp
from jax import lax
from jax.experimental import pallas as pl
from jax.experimental.pallas import tpu as pltpu
from jax.sharding import PartitionSpec as P

MESH = pl.DeviceIdType.MESH
F32 = jnp.float32
BF16 = jnp.bfloat16
HIGHEST = lax.Precision.HIGHEST
C = 64
NT = (((1,), (1,)), ((), ()))
NN = (((1,), (0,)), ((), ()))
B1, B2, B0, IM = (pl.ds(i * C, C) for i in range(4))


def fdot(a, b, dims):
    return lax.dot_general(a, b, dims, precision=HIGHEST, preferred_element_type=F32)


def places():
    s = lax.axis_index("slab")
    y = lax.axis_index("col")
    z, r = lax.div(s, 8), lax.rem(s, 8)
    rs = [r] + [lax.rem(r + d, 8) for d in range(1, 8)]
    ys = [y] + [lax.rem(y + d, 4) for d in range(1, 4)]
    zs = [z] + [lax.rem(z + d, 16) for d in range(1, 16)]
    plane = [(z * 8 + a, b) for i, a in enumerate(rs) for j, b in enumerate(ys) if i or j]
    chunk = [a * 4 + b for i, a in enumerate(rs) for j, b in enumerate(ys) if i or j]
    column = [(a * 8 + r, y) for a in zs[1:]]
    sl = [s, lax.rem(s + 1, 128), lax.rem(s + 127, 128)]
    near = [(sl[i], ys[j]) for i in (0, 1, 2) for j in (0, 1, 3) if i or j]
    return s, y, z, r * 4 + y, plane, chunk, column, near


def halo_copies(xe, rows, sems, near):
    x_src = {0: pl.ds(1, 2), 1: pl.ds(2, 1), 2: pl.ds(1, 1)}
    x_dst = {0: pl.ds(1, 2), 1: pl.ds(0, 1), 2: pl.ds(3, 1)}
    y_src = {0: pl.ds(1, 8), 1: pl.ds(8, 1), 3: pl.ds(1, 1)}
    y_dst = {0: pl.ds(1, 8), 1: pl.ds(0, 1), 3: pl.ds(9, 1)}
    out = []
    k = 0
    for i in (0, 1, 2):
        for j in (0, 1, 3):
            if i or j:
                out.append(
                    pltpu.make_async_remote_copy(
                        xe.at[x_src[i], y_src[j], rows],
                        xe.at[x_dst[i], y_dst[j], rows],
                        sems.at[0],
                        sems.at[1],
                        device_id=near[k],
                        device_id_type=MESH,
                    )
                )
                k += 1
    return out


def wait_bytes(ref, sem):
    pltpu.make_async_copy(ref, ref, sem).wait()


class Sum:
    def __init__(self, size, src, parts, tower, out, sems, place):
        self.n, self.src, self.parts, self.tower, self.out, self.sems = size, src, parts, tower, out, sems
        _, _, self.z, p, self.plane, self.chunk, self.column, _ = place
        self.mine = pl.ds(pl.multiple_of(p * size, size), size)

    def send(self, src, dst, pair, dev):
        pltpu.make_async_remote_copy(
            src, dst, self.sems.at[pair], self.sems.at[pair + 1], device_id=dev, device_id_type=MESH
        ).start()

    def scatter(self):
        for k, dev in enumerate(self.plane):
            at = pl.ds(pl.multiple_of(self.chunk[k] * self.n, self.n), self.n)
            self.send(self.src.at[at], self.parts.at[k], 0, dev)

    def climb(self):
        wait_bytes(self.parts, self.sems.at[1])
        total = self.src[self.mine, :]
        for k in range(31):
            total = total + self.parts[k]
        self.tower[self.z] = total
        for dev in self.column:
            self.send(self.tower.at[self.z], self.tower.at[self.z], 2, dev)

    def spread(self):
        wait_bytes(self.tower.at[pl.ds(0, 15)], self.sems.at[3])
        total = self.tower[0]
        for k in range(1, 16):
            total = total + self.tower[k]
        self.out[self.mine, :] = total
        for dev in self.plane:
            self.send(self.out.at[self.mine], self.out.at[self.mine], 4, dev)

    def collect(self):
        wait_bytes(self.out.at[pl.ds(0, 31 * self.n)], self.sems.at[5])

    def drain(self):
        wait_bytes(self.parts, self.sems.at[0])
        wait_bytes(self.tower.at[pl.ds(0, 15)], self.sems.at[2])
        wait_bytes(self.out.at[pl.ds(0, 31 * self.n)], self.sems.at[4])


def relayout(basis, xe, wide):
    for b, rows in ((2, B2), (0, B0), (1, B1)):
        for x in range(2):
            wide[...] = basis[b, :, x].astype(F32).reshape(C * 8, 128)
            for y in range(8):
                xe[1 + x, 1 + y, rows, :] = wide[pl.ds(y, C, stride=8), :].astype(BF16)


def coefficients(cell_map, table, coef, s, ycol):
    row = lax.broadcasted_iota(jnp.int32, (8, 128), 0)
    lane = lax.broadcasted_iota(jnp.int32, (8, 128), 1)
    one = jnp.ones((8, 128), F32)
    zero = jnp.zeros((8, 128), F32)
    y_low = jnp.where((row == 0) & (ycol == 0), zero, one)
    y_high = jnp.where((row == 7) & (ycol == 3), zero, one)
    for x in range(2):
        cells = cell_map[x]
        is_class = [cells == k for k in range(8)]
        for o in range(27):
            dx, dy, dz = o // 9, o // 3 % 3, o % 3
            c = zero
            for k in range(8):
                c = jnp.where(is_class[k], table[k, o], c)
            if dx == 0 and x == 0:
                c = jnp.where(s == 0, zero, c)
            if dx == 2 and x == 1:
                c = jnp.where(s == 127, zero, c)
            if dy == 0:
                c = c * y_low
            if dy == 2:
                c = c * y_high
            if dz == 0:
                c = pltpu.roll(jnp.where(lane == 0, zero, c), 127, 1)
            if dz == 2:
                c = pltpu.roll(jnp.where(lane == 127, zero, c), 1, 1)
            coef[pl.ds(x * 8 * 32 + o, 8, stride=32), :] = c


def stencil(xe, rows_in, rows_out, coef):
    for x in range(2):

        def body(y, carry):
            table = coef.at[pl.ds(pl.multiple_of((x * 8 + y) * 32, 32), 32)]
            acc = [jnp.zeros((C, 128), F32) for _ in range(3)]
            for dx in range(3):
                for dy in range(3):
                    piece = xe[x + dx, y + dy, rows_in, :].astype(F32)
                    for dz in range(3):
                        o = 9 * dx + 3 * dy + dz
                        acc[dz] = acc[dz] + table[o : o + 1, :] * piece
            total = acc[1] + pltpu.roll(acc[0], 1, 1) + pltpu.roll(acc[2], 127, 1)
            xe[x + 1, y + 1, rows_out, :] = total.astype(BF16)
            return carry

        lax.fori_loop(0, 8, body, 0)


def gram(xe, rows, count):
    def body(k, acc):
        x, y = k // 8, k % 8
        left = xe[x + 1, y + 1, rows, :]
        right = xe[x + 1, y + 1]
        return acc + lax.dot_general(left, right, NT, preferred_element_type=F32)

    return lax.fori_loop(0, 16, body, jnp.zeros((count, 256), F32))


def project(f_full, g):
    col = lax.broadcasted_iota(jnp.int32, (C, 256), 1)
    keep = col < 192
    first = jnp.where(keep, f_full, 0.0)
    first_b = first.astype(BF16).astype(F32)
    second = jnp.where(keep, first - fdot(first_b, g, NN), 0.0)
    second_b = second.astype(BF16).astype(F32)
    rest = jnp.where(keep, second - fdot(second_b, g, NN), 0.0)
    both = first_b + second_b
    pad = jnp.zeros((C, 256), F32)
    lane = lax.broadcasted_iota(jnp.int32, (C, 128), 1)
    row = lax.broadcasted_iota(jnp.int32, (C, 128), 0)
    own = pltpu.roll(f_full[:, 128:256], 64, 1)
    square = (
        own
        - fdot(first, jnp.concatenate([both, pad], axis=0), NT)
        - fdot(both, jnp.concatenate([rest, pad], axis=0), NT)
    )
    system = jnp.where(lane < C, square, jnp.where(lane == row + C, 1.0, 0.0))
    return first + second, both, rest, system


def factor(m):
    row = lax.broadcasted_iota(jnp.int32, (C, 128), 0)
    diag = jnp.ones((C, 128), F32)
    for j in range(C):
        top = m[j : j + 1, :]
        pivot = m[j : j + 1, j : j + 1]
        diag = jnp.where(row == j, pivot, diag)
        if j < C - 1:
            ratio = jnp.where(row > j, m[:, j : j + 1] / pivot, 0.0)
            m = m - ratio * top
    return m * lax.rsqrt(diag)


def split(v):
    high = v.astype(BF16)
    return high, (v - high.astype(F32)).astype(BF16)


def kernel(
    table, basis, cell_map,
    out_block, out_proj, out_tri,
    xe, wide, coef, src1, parts1, tower1, sum1, src2, parts2, tower2, sum2, gm, halo_sems, sum_sems,
):
    place = places()
    s, ycol, z, p, plane, chunk, column, near = place
    barrier = pltpu.get_barrier_semaphore()
    for dev in plane + column + near:
        pl.semaphore_signal(barrier, inc=1, device_id=dev, device_id_type=MESH)

    relayout(basis, xe, wide)
    coefficients(cell_map, table, coef, s, ycol)

    pl.semaphore_wait(barrier, len(plane + column + near))
    for copy in halo_copies(xe, B2, halo_sems.at[0], near):
        copy.start()
    for k, rows in ((1, B0), (2, B1)):
        for copy in halo_copies(xe, rows, halo_sems.at[k], near):
            copy.start()
    moved = xe.at[pl.ds(0, 3), pl.ds(0, 8), B2]
    wait_bytes(moved, halo_sems.at[0, 1])
    stencil(xe, B2, IM, coef)

    one = Sum(16, src1, parts1, tower1, sum1, sum_sems.at[0], place)
    two = Sum(8, src2, parts2, tower2, sum2, sum_sems.at[1], place)
    g = gram(xe, pl.ds(0, 256), 256)
    src1[0:256, :] = g[:, 0:128]
    src1[256:512, :] = g[:, 128:256]
    one.scatter()
    for copy in halo_copies(xe, IM, halo_sems.at[3], near):
        copy.start()
    one.climb()
    one.spread()
    one.collect()

    scale = 1.0 / (256 * 32 * 128)
    g = jnp.concatenate([sum1[0:256, :], sum1[256:512, :]], axis=1) * scale
    gm[...] = g
    proj, both, rest, system = project(g[192:256, :], g)
    out_proj[0] = proj

    col = lax.broadcasted_iota(jnp.int32, (C, 256), 1)
    row = lax.broadcasted_iota(jnp.int32, (C, 256), 0)
    high, low = split(jnp.where(col == row + 192, 1.0, -both))
    for k in range(4):
        wait_bytes(moved, halo_sems.at[k, 0])
        if k:
            wait_bytes(moved, halo_sems.at[k, 1])

    def correct(k, carry):
        x, y = k // 10, k % 10
        v = xe[x, y]
        w = lax.dot_general(high, v, NN, preferred_element_type=F32)
        w = w + lax.dot_general(low, v, NN, preferred_element_type=F32)
        xe[x, y, B0, :] = w.astype(BF16)
        return carry

    lax.fori_loop(0, 40, correct, 0)
    stencil(xe, B0, IM, coef)

    h = gram(xe, pl.ds(128, 128), 128)
    src2[0:128, :] = h[:, 0:128]
    src2[128:256, :] = h[:, 128:256]
    two.scatter()
    two.climb()

    done = factor(system)
    out_tri[0] = done
    inverse = pltpu.roll(done, 64, 1)[:, 0:C].astype(BF16).astype(F32)
    zero = jnp.zeros((C, C), F32)
    q_left = fdot(inverse, rest[:, 0:128], NN)
    q_own = fdot(fdot(inverse, system[:, 0:C], NN), inverse, NT)
    gm[128:192, 0:128] = q_left
    gm[0:128, 128:192] = jnp.transpose(q_left)
    gm[128:192, 128:192] = q_own
    twice = jnp.concatenate(
        [jnp.concatenate([inverse, zero], axis=1), jnp.concatenate([zero, inverse], axis=1)], axis=0
    )

    two.spread()
    two.collect()
    h = jnp.concatenate([sum2[64:128, :], sum2[192:256, :]], axis=1) * scale
    h = fdot(inverse, h, NN)
    f_full = jnp.concatenate([h[:, 0:128], fdot(h[:, 128:256], twice, NT)], axis=1)
    proj, both, rest, system = project(f_full, gm[...])
    out_proj[1] = proj
    lane = lax.broadcasted_iota(jnp.int32, (C, 128), 1)
    mixed = jnp.where(lane < C, -both[:, 128:256], jnp.where(lane == lax.broadcasted_iota(jnp.int32, (C, 128), 0) + C, 1.0, 0.0))
    mixed = fdot(mixed, twice, NN)
    high2, low2 = split(jnp.concatenate([-both[:, 0:128], mixed], axis=1))
    done = factor(system)
    out_tri[1] = done
    inverse2 = pltpu.roll(done, 64, 1)[:, 0:C].astype(BF16)
    for x in range(2):

        def finish(y, carry):
            v = xe[x + 1, y + 1]
            w = lax.dot_general(high2, v, NN, preferred_element_type=F32)
            w = w + lax.dot_general(low2, v, NN, preferred_element_type=F32)
            wide[pl.ds(y, C, stride=8), :] = lax.dot_general(inverse2, w.astype(BF16), NN, preferred_element_type=F32)
            return carry

        lax.fori_loop(0, 8, finish, 0)
        out_block[:, x] = wide[...].reshape(C, 8, 128).astype(BF16)
    one.drain()
    two.drain()


def shards(basis, cell_map, table):
    vmem = pl.BlockSpec(memory_space=pltpu.VMEM)
    block, proj, tri = pl.pallas_call(
        kernel,
        out_shape=(
            jax.ShapeDtypeStruct((C, 2, 8, 128), BF16),
            jax.ShapeDtypeStruct((2, C, 256), F32),
            jax.ShapeDtypeStruct((2, C, 128), F32),
        ),
        in_specs=[pl.BlockSpec(memory_space=pltpu.SMEM), vmem, vmem],
        out_specs=(vmem, vmem, vmem),
        scratch_shapes=[
            pltpu.VMEM((4, 10, 256, 128), BF16),
            pltpu.VMEM((C * 8, 128), F32),
            pltpu.VMEM((16 * 32, 128), F32),
            pltpu.VMEM((512, 128), F32),
            pltpu.VMEM((31, 16, 128), F32),
            pltpu.VMEM((16, 16, 128), F32),
            pltpu.VMEM((512, 128), F32),
            pltpu.VMEM((256, 128), F32),
            pltpu.VMEM((31, 8, 128), F32),
            pltpu.VMEM((16, 8, 128), F32),
            pltpu.VMEM((256, 128), F32),
            pltpu.VMEM((256, 256), F32),
            pltpu.SemaphoreType.DMA((4, 2)),
            pltpu.SemaphoreType.DMA((2, 6)),
        ],
        compiler_params=pltpu.CompilerParams(
            collective_id=0, has_side_effects=True, vmem_limit_bytes=40 * 1024 * 1024
        ),
    )(table, basis, cell_map)
    proj = jnp.swapaxes(proj, 1, 2)
    first = jnp.concatenate([proj[0, 128:192], proj[0, 0:128]], axis=0)
    lower = jnp.tril(jnp.swapaxes(tri[:, :, 0:C], 1, 2))
    return block, jnp.stack([first, proj[1, 0:192]]), lower


def solution(mesh):
    placed = (P(None, None, "slab", "col", None), P("slab", "col", None), P())
    return jax.shard_map(
        shards,
        mesh=mesh,
        in_specs=placed,
        out_specs=(P(None, "slab", "col", None), P(), P()),
        check_vma=False,
    )
```

```python
import functools

import jax
import jax.numpy as jnp
from jax import lax
from jax.experimental import pallas as pl
from jax.experimental.pallas import tpu as pltpu
from jax.sharding import PartitionSpec as P

MESH = pl.DeviceIdType.MESH
F32 = jnp.float32
BF16 = jnp.bfloat16
HIGHEST = lax.Precision.HIGHEST
C = 64
NT = (((1,), (1,)), ((), ()))
NN = (((1,), (0,)), ((), ()))
B1, B2, B0, IM = (pl.ds(i * C, C) for i in range(4))


def fdot(a, b, dims):
    return lax.dot_general(a, b, dims, precision=HIGHEST, preferred_element_type=F32)


def places():
    s = lax.axis_index("slab")
    y = lax.axis_index("col")
    z, r = lax.div(s, 8), lax.rem(s, 8)
    rs = [r] + [lax.rem(r + d, 8) for d in range(1, 8)]
    ys = [y] + [lax.rem(y + d, 4) for d in range(1, 4)]
    zs = [z] + [lax.rem(z + d, 16) for d in range(1, 16)]
    plane = [(z * 8 + a, b) for i, a in enumerate(rs) for j, b in enumerate(ys) if i or j]
    chunk = [a * 4 + b for i, a in enumerate(rs) for j, b in enumerate(ys) if i or j]
    column = [(a * 8 + r, y) for a in zs[1:]]
    sl = [s, lax.rem(s + 1, 128), lax.rem(s + 127, 128)]
    near = [(sl[i], ys[j]) for i in (0, 1, 2) for j in (0, 1, 3) if i or j]
    return s, y, z, r * 4 + y, plane, chunk, column, near


def halo_copies(xe, rows, sems, near):
    x_src = {0: pl.ds(1, 2), 1: pl.ds(2, 1), 2: pl.ds(1, 1)}
    x_dst = {0: pl.ds(1, 2), 1: pl.ds(0, 1), 2: pl.ds(3, 1)}
    y_src = {0: pl.ds(1, 8), 1: pl.ds(8, 1), 3: pl.ds(1, 1)}
    y_dst = {0: pl.ds(1, 8), 1: pl.ds(0, 1), 3: pl.ds(9, 1)}
    out = []
    k = 0
    for i in (0, 1, 2):
        for j in (0, 1, 3):
            if i or j:
                out.append(
                    pltpu.make_async_remote_copy(
                        xe.at[x_src[i], y_src[j], rows],
                        xe.at[x_dst[i], y_dst[j], rows],
                        sems.at[0],
                        sems.at[1],
                        device_id=near[k],
                        device_id_type=MESH,
                    )
                )
                k += 1
    return out


def wait_bytes(ref, sem):
    pltpu.make_async_copy(ref, ref, sem).wait()


class Sum:
    def __init__(self, src, parts, tower, out, sems, place):
        self.src, self.parts, self.tower, self.out, self.sems = src, parts, tower, out, sems
        _, _, self.z, self.mine, self.plane, self.chunk, self.column, _ = place

    def send(self, src, dst, pair, dev):
        pltpu.make_async_remote_copy(
            src, dst, self.sems.at[pair], self.sems.at[pair + 1], device_id=dev, device_id_type=MESH
        ).start()

    def scatter(self):
        for k, dev in enumerate(self.plane):
            self.send(self.src.at[self.chunk[k]], self.parts.at[k], 0, dev)

    def climb(self):
        wait_bytes(self.parts, self.sems.at[1])
        total = self.src[self.mine]
        for k in range(31):
            total = total + self.parts[k]
        self.tower[self.z] = total
        for dev in self.column:
            self.send(self.tower.at[self.z], self.tower.at[self.z], 2, dev)

    def spread(self):
        wait_bytes(self.tower.at[pl.ds(0, 15)], self.sems.at[3])
        total = self.tower[0]
        for k in range(1, 16):
            total = total + self.tower[k]
        self.out[self.mine] = total
        for dev in self.plane:
            self.send(self.out.at[self.mine], self.out.at[self.mine], 4, dev)

    def collect(self):
        wait_bytes(self.out.at[pl.ds(0, 31)], self.sems.at[5])

    def drain(self):
        wait_bytes(self.parts, self.sems.at[0])
        wait_bytes(self.tower.at[pl.ds(0, 15)], self.sems.at[2])
        wait_bytes(self.out.at[pl.ds(0, 31)], self.sems.at[4])


def relayout(basis, xe, wide):
    for b, rows in ((2, B2), (0, B0), (1, B1)):
        for x in range(2):
            wide[...] = basis[b, :, x].astype(F32).reshape(C * 8, 128)
            for y in range(8):
                xe[1 + x, 1 + y, rows, :] = wide[pl.ds(y, C, stride=8), :].astype(BF16)


def coefficients(cell_map, table, coef, s, ycol):
    row = lax.broadcasted_iota(jnp.int32, (8, 128), 0)
    lane = lax.broadcasted_iota(jnp.int32, (8, 128), 1)
    one = jnp.ones((8, 128), F32)
    zero = jnp.zeros((8, 128), F32)
    y_low = jnp.where((row == 0) & (ycol == 0), zero, one)
    y_high = jnp.where((row == 7) & (ycol == 3), zero, one)
    for x in range(2):
        cells = cell_map[x]
        is_class = [cells == k for k in range(8)]
        for o in range(27):
            dx, dy, dz = o // 9, o // 3 % 3, o % 3
            c = zero
            for k in range(8):
                c = jnp.where(is_class[k], table[k, o], c)
            if dx == 0 and x == 0:
                c = jnp.where(s == 0, zero, c)
            if dx == 2 and x == 1:
                c = jnp.where(s == 127, zero, c)
            if dy == 0:
                c = c * y_low
            if dy == 2:
                c = c * y_high
            if dz == 0:
                c = pltpu.roll(jnp.where(lane == 0, zero, c), 127, 1)
            if dz == 2:
                c = pltpu.roll(jnp.where(lane == 127, zero, c), 1, 1)
            coef[pl.ds(x * 8 * 32 + o, 8, stride=32), :] = c


def stencil(xe, rows_in, rows_out, coef):
    for x in range(2):

        def body(y, carry):
            table = coef.at[pl.ds(pl.multiple_of((x * 8 + y) * 32, 32), 32)]
            acc = [jnp.zeros((C, 128), F32) for _ in range(3)]
            for dx in range(3):
                for dy in range(3):
                    piece = xe[x + dx, y + dy, rows_in, :].astype(F32)
                    for dz in range(3):
                        o = 9 * dx + 3 * dy + dz
                        acc[dz] = acc[dz] + table[o : o + 1, :] * piece
            total = acc[1] + pltpu.roll(acc[0], 1, 1) + pltpu.roll(acc[2], 127, 1)
            xe[x + 1, y + 1, rows_out, :] = total.astype(BF16)
            return carry

        lax.fori_loop(0, 8, body, 0)


def own_planes(xe, rows):
    return jnp.concatenate([xe[1 + x, 1 + y, rows, :] for x in range(2) for y in range(8)], axis=1)


def gram(left, right):
    return lax.dot_general(left, right, NT, preferred_element_type=F32)


def pack(src, k, v):
    size = src.shape[1]
    for i in range(v.shape[0] // size):
        src[k + i] = v[i * size : (i + 1) * size]


def project(f_full, g):
    col = lax.broadcasted_iota(jnp.int32, (C, 256), 1)
    keep = col < 192
    first = jnp.where(keep, f_full, 0.0)
    first_b = first.astype(BF16).astype(F32)
    second = jnp.where(keep, first - fdot(first_b, g, NN), 0.0)
    second_b = second.astype(BF16).astype(F32)
    rest = jnp.where(keep, second - fdot(second_b, g, NN), 0.0)
    both = first_b + second_b
    pad = jnp.zeros((C, 256), F32)
    lane = lax.broadcasted_iota(jnp.int32, (C, 128), 1)
    own = pltpu.roll(f_full[:, 128:256], 64, 1)
    square = (
        own
        - fdot(first, jnp.concatenate([both, pad], axis=0), NT)
        - fdot(both, jnp.concatenate([rest, pad], axis=0), NT)
    )
    system = jnp.where(lane < C, square, 0.0)
    return first + second, both, rest, system


def splat(v, lane):
    return jnp.broadcast_to(v[:, lane:lane + 1], (8, 128))


def eliminate(m):
    sub = lax.broadcasted_iota(jnp.int32, (8, 128), 0)
    out = [None] * 8
    for j in range(0, 64, 4):
        t, q = j // 8, j % 8
        r = [jnp.broadcast_to(m[t][q + a : q + a + 1, :], (8, 128)) for a in range(4)]
        p = [[splat(r[a], j + b) if b >= a else None for b in range(4)] for a in range(4)]
        det = p[0][0] * p[1][1] - p[0][1] * p[0][1]
        inv = 1.0 / det
        y = [[(p[1][1] * p[0][b] - p[0][1] * p[1][b]) * inv, (p[0][0] * p[1][b] - p[0][1] * p[0][b]) * inv] for b in (2, 3)]
        s22 = p[2][2] - p[0][2] * y[0][0] - p[1][2] * y[0][1]
        s23 = p[2][3] - p[0][2] * y[1][0] - p[1][2] * y[1][1]
        s33 = p[3][3] - p[0][3] * y[1][0] - p[1][3] * y[1][1]
        det2 = s22 * s33 - s23 * s23
        r2 = r[2] - y[0][0] * r[0] - y[0][1] * r[1]
        r3 = r[3] - y[1][0] * r[0] - y[1][1] * r[1]
        if j < 60:
            inv2 = 1.0 / det2
            x0 = (p[1][1] * r[0] - p[0][1] * r[1]) * inv
            x1 = (p[0][0] * r[1] - p[0][1] * r[0]) * inv
            x2 = (s33 * r2 - s23 * r3) * inv2
            x3 = (s22 * r3 - s23 * r2) * inv2
            x0 = x0 - y[0][0] * x2 - y[1][0] * x3
            x1 = x1 - y[0][1] * x2 - y[1][1] * x3
            for v in range(t if q == 0 else t + 1, 8):
                c = [splat(m[v], j + b) for b in range(4)]
                new = m[v] - (c[0] * x0 + c[1] * x1) - (c[2] * x2 + c[3] * x3)
                m[v] = jnp.where(sub >= 4, new, m[v]) if v == t else new
        a0 = lax.rsqrt(p[0][0])
        a1 = lax.rsqrt(det * (1.0 / p[0][0]))
        a2 = lax.rsqrt(s22)
        a3 = lax.rsqrt(det2 * (1.0 / s22))
        u = [r[0] * a0, (r[1] - (p[0][1] * (1.0 / p[0][0])) * r[0]) * a1, r2 * a2, (r3 - (s23 * (1.0 / s22)) * r2) * a3]
        o = out[t] if q else u[3]
        for a in range(4):
            o = jnp.where(sub == q + a, u[a], o)
        out[t] = o
    return out


def factor(system):
    row = lax.broadcasted_iota(jnp.int32, (C, 128), 0)
    lane = lax.broadcasted_iota(jnp.int32, (C, 128), 1)
    diag = jnp.where(lane == row, system, 0.0)
    across = jnp.sum(diag, axis=1, keepdims=True)
    along = jnp.sum(diag, axis=0, keepdims=True)
    scale = lax.rsqrt(across)
    unit = lax.rsqrt(along)
    m = jnp.where(lane < C, system * scale * unit, jnp.where(lane == row + C, scale, 0.0))
    m = jnp.concatenate(eliminate([m[8 * v : 8 * v + 8] for v in range(8)]), axis=0)
    return jnp.where(lane < C, m * (along * unit), m)


def split(v):
    high = v.astype(BF16)
    return high, (v - high.astype(F32)).astype(BF16)


def mixed(weights, v):
    w = lax.dot_general(jnp.concatenate(weights, axis=0), v, NN, preferred_element_type=F32)
    return (w[0:C] + w[C : 2 * C]).astype(BF16)


def kernel(
    table, basis, cell_map,
    out_block, out_proj, out_tri,
    xe, wide, coef, gm,
    src0, parts0, tower0, sum0, src1, parts1, tower1, sum1, src2, parts2, tower2, sum2,
    halo_sems, sum_sems,
):
    place = places()
    s, ycol, z, p, plane, chunk, column, near = place
    barrier = pltpu.get_barrier_semaphore()
    for dev in plane + column + near:
        pl.semaphore_signal(barrier, inc=1, device_id=dev, device_id_type=MESH)
    zero = Sum(src0, parts0, tower0, sum0, sum_sems.at[0], place)
    one = Sum(src1, parts1, tower1, sum1, sum_sems.at[1], place)
    two = Sum(src2, parts2, tower2, sum2, sum_sems.at[2], place)

    relayout(basis, xe, wide)
    coefficients(cell_map, table, coef, s, ycol)
    v = own_planes(xe, pl.ds(0, 192))
    g = gram(v, v[0:128])
    pack(src0, 0, g)
    g = gram(v[128:192], v[128:192])
    pack(src0, 24, jnp.concatenate([g, g], axis=1))

    pl.semaphore_wait(barrier, len(plane + column + near))
    for copy in halo_copies(xe, B2, halo_sems.at[0], near):
        copy.start()
    zero.scatter()
    moved = xe.at[pl.ds(0, 3), pl.ds(0, 8), B2]
    wait_bytes(moved, halo_sems.at[0, 1])
    stencil(xe, B2, IM, coef)

    x = own_planes(xe, pl.ds(0, 256))
    f = gram(x[192:256], x)
    pack(src1, 0, f[:, 0:128])
    pack(src1, 16, f[:, 128:256])
    one.scatter()
    zero.climb()
    for k, rows in ((1, B0), (2, B1), (3, IM)):
        for copy in halo_copies(xe, rows, halo_sems.at[k], near):
            copy.start()
    one.climb()
    zero.spread()
    one.spread()
    zero.collect()
    one.collect()

    scale = 1.0 / (256 * 32 * 128)
    gm[0:192, 0:128] = sum0[0:24].reshape(192, 128) * scale
    gm[0:128, 128:192] = jnp.transpose(gm[128:192, 0:128])
    gm[0:192, 192:256] = jnp.zeros((192, 64), F32)
    gm[192:256, :] = jnp.zeros((64, 256), F32)
    gm[128:192, 128:192] = sum0[24:32].reshape(64, 128)[:, 0:64] * scale
    f = jnp.concatenate([sum1[0:16].reshape(64, 128), sum1[16:32].reshape(64, 128)], axis=1) * scale
    proj, both, rest, system = project(f, gm[...])
    out_proj[0] = proj

    col = lax.broadcasted_iota(jnp.int32, (C, 256), 1)
    row = lax.broadcasted_iota(jnp.int32, (C, 256), 0)
    weights = split(jnp.where(col == row + 192, 1.0, -both))
    for k in range(4):
        wait_bytes(moved, halo_sems.at[k, 0])
        if k:
            wait_bytes(moved, halo_sems.at[k, 1])

    def correct(x, carry):
        v = jnp.concatenate([xe[x, y] for y in range(10)], axis=1)
        w = mixed(weights, v)
        for y in range(10):
            xe[x, y, B0, :] = w[:, y * 128 : (y + 1) * 128]
        return carry

    lax.fori_loop(0, 4, correct, 0)
    stencil(xe, B0, IM, coef)

    x = own_planes(xe, pl.ds(0, 256))
    h = gram(x[192:256], x)
    pack(src2, 0, h[:, 0:128])
    pack(src2, 16, h[:, 128:256])
    two.scatter()
    two.climb()

    done = factor(system)
    out_tri[0] = done
    inverse = pltpu.roll(done, 64, 1)[:, 0:C].astype(BF16).astype(F32)
    none = jnp.zeros((C, C), F32)
    q_left = fdot(inverse, rest[:, 0:128], NN)
    q_own = fdot(fdot(inverse, system[:, 0:C], NN), inverse, NT)
    gm[128:192, 0:128] = q_left
    gm[0:128, 128:192] = jnp.transpose(q_left)
    gm[128:192, 128:192] = q_own
    twice = jnp.concatenate(
        [jnp.concatenate([inverse, none], axis=1), jnp.concatenate([none, inverse], axis=1)], axis=0
    )

    two.spread()
    two.collect()
    h = jnp.concatenate([sum2[0:16].reshape(64, 128), sum2[16:32].reshape(64, 128)], axis=1) * scale
    h = fdot(inverse, h, NN)
    f = jnp.concatenate([h[:, 0:128], fdot(h[:, 128:256], twice, NT)], axis=1)
    proj, both, rest, system = project(f, gm[...])
    out_proj[1] = proj
    lane = lax.broadcasted_iota(jnp.int32, (C, 128), 1)
    unit = lax.broadcasted_iota(jnp.int32, (C, 128), 0) + C
    right = fdot(jnp.where(lane < C, -both[:, 128:256], jnp.where(lane == unit, 1.0, 0.0)), twice, NN)
    weights = split(jnp.concatenate([-both[:, 0:128], right], axis=1))
    w = mixed(weights, own_planes(xe, pl.ds(0, 256)))
    done = factor(system)
    out_tri[1] = done
    inverse = pltpu.roll(done, 64, 1)[:, 0:C].astype(BF16)
    q = lax.dot_general(inverse, w, NN, preferred_element_type=F32)
    for x in range(2):
        for y in range(8):
            k = (x * 8 + y) * 128
            wide[pl.ds(y, C, stride=8), :] = q[:, k : k + 128]
        out_block[:, x] = wide[...].reshape(C, 8, 128).astype(BF16)
    zero.drain()
    one.drain()
    two.drain()


def sum_scratch(size):
    return [pltpu.VMEM((count, size, 128), F32) for count in (32, 31, 16, 32)]


def shards(basis, cell_map, table):
    vmem = pl.BlockSpec(memory_space=pltpu.VMEM)
    block, proj, tri = pl.pallas_call(
        kernel,
        out_shape=(
            jax.ShapeDtypeStruct((C, 2, 8, 128), BF16),
            jax.ShapeDtypeStruct((2, C, 256), F32),
            jax.ShapeDtypeStruct((2, C, 128), F32),
        ),
        in_specs=[pl.BlockSpec(memory_space=pltpu.SMEM), vmem, vmem],
        out_specs=(vmem, vmem, vmem),
        scratch_shapes=[
            pltpu.VMEM((4, 10, 256, 128), BF16),
            pltpu.VMEM((C * 8, 128), F32),
            pltpu.VMEM((16 * 32, 128), F32),
            pltpu.VMEM((256, 256), F32),
            *sum_scratch(8),
            *sum_scratch(4),
            *sum_scratch(4),
            pltpu.SemaphoreType.DMA((4, 2)),
            pltpu.SemaphoreType.DMA((3, 6)),
        ],
        compiler_params=pltpu.CompilerParams(
            collective_id=0, has_side_effects=True, vmem_limit_bytes=40 * 1024 * 1024
        ),
    )(table, basis, cell_map)
    proj = jnp.swapaxes(proj, 1, 2)
    first = jnp.concatenate([proj[0, 128:192], proj[0, 0:128]], axis=0)
    lower = jnp.tril(jnp.swapaxes(tri[:, :, 0:C], 1, 2))
    return block, jnp.stack([first, proj[1, 0:192]]), lower


def solution(mesh):
    placed = (P(None, None, "slab", "col", None), P("slab", "col", None), P())
    return jax.shard_map(
        shards,
        mesh=mesh,
        in_specs=placed,
        out_specs=(P(None, "slab", "col", None), P(), P()),
        check_vma=False,
    )
```

```python
import functools

import jax
import jax.numpy as jnp
from jax import lax
from jax.experimental import pallas as pl
from jax.experimental.pallas import tpu as pltpu
from jax.sharding import PartitionSpec as P

MESH = pl.DeviceIdType.MESH
F32 = jnp.float32
BF16 = jnp.bfloat16
HIGHEST = lax.Precision.HIGHEST
C = 64
NT = (((1,), (1,)), ((), ()))
NN = (((1,), (0,)), ((), ()))
B1, B2, B0, IM = (pl.ds(i * C, C) for i in range(4))


def fdot(a, b, dims):
    return lax.dot_general(a, b, dims, precision=HIGHEST, preferred_element_type=F32)


def places():
    s = lax.axis_index("slab")
    y = lax.axis_index("col")
    z, r = lax.div(s, 8), lax.rem(s, 8)
    rs = [r] + [lax.rem(r + d, 8) for d in range(1, 8)]
    ys = [y] + [lax.rem(y + d, 4) for d in range(1, 4)]
    zs = [z] + [lax.rem(z + d, 16) for d in range(1, 16)]
    plane = [(z * 8 + a, b) for i, a in enumerate(rs) for j, b in enumerate(ys) if i or j]
    chunk = [a * 4 + b for i, a in enumerate(rs) for j, b in enumerate(ys) if i or j]
    column = [(a * 8 + r, y) for a in zs[1:]]
    sl = [s, lax.rem(s + 1, 128), lax.rem(s + 127, 128)]
    near = [(sl[i], ys[j]) for i in (0, 1, 2) for j in (0, 1, 3) if i or j]
    return s, y, z, r * 4 + y, plane, chunk, column, near


def halo_copies(xe, rows, sems, near):
    x_src = {0: pl.ds(1, 2), 1: pl.ds(2, 1), 2: pl.ds(1, 1)}
    x_dst = {0: pl.ds(1, 2), 1: pl.ds(0, 1), 2: pl.ds(3, 1)}
    y_src = {0: pl.ds(1, 8), 1: pl.ds(8, 1), 3: pl.ds(1, 1)}
    y_dst = {0: pl.ds(1, 8), 1: pl.ds(0, 1), 3: pl.ds(9, 1)}
    out = []
    k = 0
    for i in (0, 1, 2):
        for j in (0, 1, 3):
            if i or j:
                out.append(
                    pltpu.make_async_remote_copy(
                        xe.at[x_src[i], y_src[j], rows],
                        xe.at[x_dst[i], y_dst[j], rows],
                        sems.at[0],
                        sems.at[1],
                        device_id=near[k],
                        device_id_type=MESH,
                    )
                )
                k += 1
    return out


def wait_bytes(ref, sem):
    pltpu.make_async_copy(ref, ref, sem).wait()


class Sum:
    def __init__(self, src, parts, tower, out, sems, place):
        self.src, self.parts, self.tower, self.out, self.sems = src, parts, tower, out, sems
        _, _, self.z, self.mine, self.plane, self.chunk, self.column, _ = place

    def send(self, src, dst, pair, dev):
        pltpu.make_async_remote_copy(
            src, dst, self.sems.at[pair], self.sems.at[pair + 1], device_id=dev, device_id_type=MESH
        ).start()

    def scatter(self):
        for k, dev in enumerate(self.plane):
            self.send(self.src.at[self.chunk[k]], self.parts.at[k], 0, dev)

    def climb(self):
        wait_bytes(self.parts, self.sems.at[1])
        total = self.src[self.mine]
        for k in range(31):
            total = total + self.parts[k]
        self.tower[self.z] = total
        for dev in self.column:
            self.send(self.tower.at[self.z], self.tower.at[self.z], 2, dev)

    def spread(self):
        wait_bytes(self.tower.at[pl.ds(0, 15)], self.sems.at[3])
        total = self.tower[0]
        for k in range(1, 16):
            total = total + self.tower[k]
        self.out[self.mine] = total
        for dev in self.plane:
            self.send(self.out.at[self.mine], self.out.at[self.mine], 4, dev)

    def collect(self):
        wait_bytes(self.out.at[pl.ds(0, 31)], self.sems.at[5])

    def drain(self):
        wait_bytes(self.parts, self.sems.at[0])
        wait_bytes(self.tower.at[pl.ds(0, 15)], self.sems.at[2])
        wait_bytes(self.out.at[pl.ds(0, 31)], self.sems.at[4])


def relayout(basis, xe, wide):
    for b, rows in ((2, B2), (0, B0), (1, B1)):
        for x in range(2):
            wide[...] = basis[b, :, x].astype(F32).reshape(C * 8, 128)
            for y in range(8):
                xe[1 + x, 1 + y, rows, :] = wide[pl.ds(y, C, stride=8), :].astype(BF16)


def coefficients(cell_map, table, coef, s, ycol):
    row = lax.broadcasted_iota(jnp.int32, (8, 128), 0)
    lane = lax.broadcasted_iota(jnp.int32, (8, 128), 1)
    one = jnp.ones((8, 128), F32)
    zero = jnp.zeros((8, 128), F32)
    y_low = jnp.where((row == 0) & (ycol == 0), zero, one)
    y_high = jnp.where((row == 7) & (ycol == 3), zero, one)
    for x in range(2):
        cells = cell_map[x]
        is_class = [cells == k for k in range(8)]
        for o in range(27):
            dx, dy, dz = o // 9, o // 3 % 3, o % 3
            c = zero
            for k in range(8):
                c = jnp.where(is_class[k], table[k, o], c)
            if dx == 0 and x == 0:
                c = jnp.where(s == 0, zero, c)
            if dx == 2 and x == 1:
                c = jnp.where(s == 127, zero, c)
            if dy == 0:
                c = c * y_low
            if dy == 2:
                c = c * y_high
            if dz == 0:
                c = pltpu.roll(jnp.where(lane == 0, zero, c), 127, 1)
            if dz == 2:
                c = pltpu.roll(jnp.where(lane == 127, zero, c), 1, 1)
            coef[pl.ds(x * 8 * 32 + o, 8, stride=32), :] = c


def is_own(x, y):
    return x in (1, 2) and 1 <= y <= 8


def stencil(xe, rows_in, rows_out, coef, held=None, local=None):
    for x in range(2):
        for y in range(8):
            table = coef.at[pl.ds((x * 8 + y) * 32, 32)]
            acc = [None, None, None]
            if local is False:
                acc = [held[x * 8 + y, dz] for dz in range(3)]
            for dx in range(3):
                for dy in range(3):
                    if local is not None and is_own(x + dx, y + dy) != local:
                        continue
                    piece = xe[x + dx, y + dy, rows_in, :].astype(F32)
                    for dz in range(3):
                        o = 9 * dx + 3 * dy + dz
                        term = table[o : o + 1, :] * piece
                        acc[dz] = term if acc[dz] is None else acc[dz] + term
            if local:
                for dz in range(3):
                    held[x * 8 + y, dz] = acc[dz]
            else:
                total = acc[1] + pltpu.roll(acc[0], 1, 1) + pltpu.roll(acc[2], 127, 1)
                xe[x + 1, y + 1, rows_out, :] = total.astype(BF16)


def own_planes(xe, rows):
    return jnp.concatenate([xe[1 + x, 1 + y, rows, :] for x in range(2) for y in range(8)], axis=1)


def gram(left, right):
    return lax.dot_general(left, right, NT, preferred_element_type=F32)


def pack(src, k, v):
    size = src.shape[1]
    for i in range(v.shape[0] // size):
        src[k + i] = v[i * size : (i + 1) * size]


def project(f_full, g):
    col = lax.broadcasted_iota(jnp.int32, (C, 256), 1)
    keep = col < 192
    first = jnp.where(keep, f_full, 0.0)
    first_b = first.astype(BF16).astype(F32)
    second = jnp.where(keep, first - fdot(first_b, g, NN), 0.0)
    second_b = second.astype(BF16).astype(F32)
    rest = jnp.where(keep, second - fdot(second_b, g, NN), 0.0)
    both = first_b + second_b
    pad = jnp.zeros((C, 256), F32)
    lane = lax.broadcasted_iota(jnp.int32, (C, 128), 1)
    own = pltpu.roll(f_full[:, 128:256], 64, 1)
    square = (
        own
        - fdot(first, jnp.concatenate([both, pad], axis=0), NT)
        - fdot(both, jnp.concatenate([rest, pad], axis=0), NT)
    )
    system = jnp.where(lane < C, square, 0.0)
    return first + second, both, rest, system


def splat(v, lane):
    return jnp.broadcast_to(v[:, lane:lane + 1], (8, 128))


def eliminate(m):
    sub = lax.broadcasted_iota(jnp.int32, (8, 128), 0)
    out = [None] * 8
    for j in range(0, 64, 4):
        t, q = j // 8, j % 8
        r = [jnp.broadcast_to(m[t][q + a : q + a + 1, :], (8, 128)) for a in range(4)]
        p = [[splat(r[a], j + b) if b >= a else None for b in range(4)] for a in range(4)]
        det = p[0][0] * p[1][1] - p[0][1] * p[0][1]
        inv = 1.0 / det
        y = [[(p[1][1] * p[0][b] - p[0][1] * p[1][b]) * inv, (p[0][0] * p[1][b] - p[0][1] * p[0][b]) * inv] for b in (2, 3)]
        s22 = p[2][2] - p[0][2] * y[0][0] - p[1][2] * y[0][1]
        s23 = p[2][3] - p[0][2] * y[1][0] - p[1][2] * y[1][1]
        s33 = p[3][3] - p[0][3] * y[1][0] - p[1][3] * y[1][1]
        det2 = s22 * s33 - s23 * s23
        r2 = r[2] - y[0][0] * r[0] - y[0][1] * r[1]
        r3 = r[3] - y[1][0] * r[0] - y[1][1] * r[1]
        if j < 60:
            inv2 = 1.0 / det2
            x0 = (p[1][1] * r[0] - p[0][1] * r[1]) * inv
            x1 = (p[0][0] * r[1] - p[0][1] * r[0]) * inv
            x2 = (s33 * r2 - s23 * r3) * inv2
            x3 = (s22 * r3 - s23 * r2) * inv2
            x0 = x0 - y[0][0] * x2 - y[1][0] * x3
            x1 = x1 - y[0][1] * x2 - y[1][1] * x3
            for v in range(t if q == 0 else t + 1, 8):
                c = [splat(m[v], j + b) for b in range(4)]
                new = m[v] - (c[0] * x0 + c[1] * x1) - (c[2] * x2 + c[3] * x3)
                m[v] = jnp.where(sub >= 4, new, m[v]) if v == t else new
        a0 = lax.rsqrt(p[0][0])
        a1 = lax.rsqrt(det * (1.0 / p[0][0]))
        a2 = lax.rsqrt(s22)
        a3 = lax.rsqrt(det2 * (1.0 / s22))
        u = [r[0] * a0, (r[1] - (p[0][1] * (1.0 / p[0][0])) * r[0]) * a1, r2 * a2, (r3 - (s23 * (1.0 / s22)) * r2) * a3]
        o = out[t] if q else u[3]
        for a in range(4):
            o = jnp.where(sub == q + a, u[a], o)
        out[t] = o
    return out


def factor(system):
    row = lax.broadcasted_iota(jnp.int32, (C, 128), 0)
    lane = lax.broadcasted_iota(jnp.int32, (C, 128), 1)
    diag = jnp.where(lane == row, system, 0.0)
    across = jnp.sum(diag, axis=1, keepdims=True)
    along = jnp.sum(diag, axis=0, keepdims=True)
    scale = lax.rsqrt(across)
    unit = lax.rsqrt(along)
    m = jnp.where(lane < C, system * scale * unit, jnp.where(lane == row + C, scale, 0.0))
    m = jnp.concatenate(eliminate([m[8 * v : 8 * v + 8] for v in range(8)]), axis=0)
    return jnp.where(lane < C, m * (along * unit), m)


def split(v):
    high = v.astype(BF16)
    return high, (v - high.astype(F32)).astype(BF16)


def mixed(weights, v):
    w = lax.dot_general(jnp.concatenate(weights, axis=0), v, NN, preferred_element_type=F32)
    return (w[0:C] + w[C : 2 * C]).astype(BF16)


def kernel(
    table_hbm, basis_hbm, map_hbm,
    w_hbm, proj_hbm, tri_hbm,
    out_w, out_proj, out_tri, table, basis, cell_map, xe, wide, coef, held, gm,
    src0, parts0, tower0, sum0, src1, parts1, tower1, sum1, src2, parts2, tower2, sum2,
    halo_sems, sum_sems, in_sems, out_sems,
):
    place = places()
    s, ycol, z, p, plane, chunk, column, near = place
    barrier = pltpu.get_barrier_semaphore()
    for dev in plane + column + near:
        pl.semaphore_signal(barrier, inc=1, device_id=dev, device_id_type=MESH)
    loads = [
        pltpu.make_async_copy(basis_hbm, basis, in_sems.at[0]),
        pltpu.make_async_copy(map_hbm, cell_map, in_sems.at[1]),
        pltpu.make_async_copy(table_hbm, table, in_sems.at[2]),
    ]
    for load in loads:
        load.start()
    zero = Sum(src0, parts0, tower0, sum0, sum_sems.at[0], place)
    one = Sum(src1, parts1, tower1, sum1, sum_sems.at[1], place)
    two = Sum(src2, parts2, tower2, sum2, sum_sems.at[2], place)

    loads[0].wait()
    relayout(basis, xe, wide)
    loads[1].wait()
    loads[2].wait()
    coefficients(cell_map, table, coef, s, ycol)
    v = own_planes(xe, pl.ds(0, 192))
    g = gram(v, v[0:128])
    pack(src0, 0, g)
    g = gram(v[128:192], v[128:192])
    pack(src0, 24, jnp.concatenate([g, g], axis=1))

    stencil(xe, B2, IM, coef, held, True)
    pl.semaphore_wait(barrier, len(plane + column + near))
    for copy in halo_copies(xe, B2, halo_sems.at[0], near):
        copy.start()
    zero.scatter()
    moved = xe.at[pl.ds(0, 3), pl.ds(0, 8), B2]
    wait_bytes(moved, halo_sems.at[0, 1])
    stencil(xe, B2, IM, coef, held, False)

    x = own_planes(xe, pl.ds(0, 256))
    f = gram(x[192:256], x)
    pack(src1, 0, f[:, 0:128])
    pack(src1, 16, f[:, 128:256])
    one.scatter()
    zero.climb()
    for k, rows in ((1, B0), (2, B1), (3, IM)):
        for copy in halo_copies(xe, rows, halo_sems.at[k], near):
            copy.start()
    one.climb()
    zero.spread()
    one.spread()
    zero.collect()
    one.collect()

    scale = 1.0 / (256 * 32 * 128)
    gm[0:192, 0:128] = sum0[0:24].reshape(192, 128) * scale
    gm[0:128, 128:192] = jnp.transpose(gm[128:192, 0:128])
    gm[0:192, 192:256] = jnp.zeros((192, 64), F32)
    gm[192:256, :] = jnp.zeros((64, 256), F32)
    gm[128:192, 128:192] = sum0[24:32].reshape(64, 128)[:, 0:64] * scale
    f = jnp.concatenate([sum1[0:16].reshape(64, 128), sum1[16:32].reshape(64, 128)], axis=1) * scale
    proj, both, rest, system = project(f, gm[...])
    out_proj[0] = proj

    col = lax.broadcasted_iota(jnp.int32, (C, 256), 1)
    row = lax.broadcasted_iota(jnp.int32, (C, 256), 0)
    weights = split(jnp.where(col == row + 192, 1.0, -both))
    for k in range(4):
        wait_bytes(moved, halo_sems.at[k, 0])
        if k:
            wait_bytes(moved, halo_sems.at[k, 1])

    def correct(x, carry):
        v = jnp.concatenate([xe[x, y] for y in range(10)], axis=1)
        w = mixed(weights, v)
        for y in range(10):
            xe[x, y, B0, :] = w[:, y * 128 : (y + 1) * 128]
        return carry

    lax.fori_loop(0, 4, correct, 0)
    stencil(xe, B0, IM, coef)

    x = own_planes(xe, pl.ds(0, 256))
    h = gram(x[192:256], x)
    pack(src2, 0, h[:, 0:128])
    pack(src2, 16, h[:, 128:256])
    two.scatter()
    two.climb()

    done = factor(system)
    out_tri[0] = done
    inverse = pltpu.roll(done, 64, 1)[:, 0:C].astype(BF16).astype(F32)
    none = jnp.zeros((C, C), F32)
    q_left = fdot(inverse, rest[:, 0:128], NN)
    q_own = fdot(fdot(inverse, system[:, 0:C], NN), inverse, NT)
    gm[128:192, 0:128] = q_left
    gm[0:128, 128:192] = jnp.transpose(q_left)
    gm[128:192, 128:192] = q_own
    twice = jnp.concatenate(
        [jnp.concatenate([inverse, none], axis=1), jnp.concatenate([none, inverse], axis=1)], axis=0
    )

    two.spread()
    two.collect()
    h = jnp.concatenate([sum2[0:16].reshape(64, 128), sum2[16:32].reshape(64, 128)], axis=1) * scale
    h = fdot(inverse, h, NN)
    f = jnp.concatenate([h[:, 0:128], fdot(h[:, 128:256], twice, NT)], axis=1)
    proj, both, rest, system = project(f, gm[...])
    out_proj[1] = proj
    lane = lax.broadcasted_iota(jnp.int32, (C, 128), 1)
    unit = lax.broadcasted_iota(jnp.int32, (C, 128), 0) + C
    right = fdot(jnp.where(lane < C, -both[:, 128:256], jnp.where(lane == unit, 1.0, 0.0)), twice, NN)
    weights = split(jnp.concatenate([-both[:, 0:128], right], axis=1))
    out_w[...] = mixed(weights, own_planes(xe, pl.ds(0, 256)))
    stores = [
        pltpu.make_async_copy(out_proj, proj_hbm, out_sems.at[0]),
        pltpu.make_async_copy(out_w, w_hbm, out_sems.at[1]),
        pltpu.make_async_copy(out_tri, tri_hbm, out_sems.at[2]),
    ]
    stores[0].start()
    stores[1].start()
    out_tri[1] = factor(system)
    stores[2].start()
    zero.drain()
    one.drain()
    two.drain()
    for store in stores:
        store.wait()


def finish(w_hbm, proj_hbm, tri_hbm, out_block, out_proj, out_tri, w, proj, tri, wide, sems):
    loads = [
        pltpu.make_async_copy(tri_hbm, tri, sems.at[0]),
        pltpu.make_async_copy(w_hbm, w, sems.at[1]),
        pltpu.make_async_copy(proj_hbm, proj, sems.at[2]),
    ]
    for load in loads:
        load.start()
    for load in loads:
        load.wait()
    inverse = pltpu.roll(tri[1], 64, 1)[:, 0:C].astype(BF16)
    q = lax.dot_general(inverse, w[...], NN, preferred_element_type=F32)
    for x in range(2):
        for y in range(8):
            k = (x * 8 + y) * 128
            wide[pl.ds(y, C, stride=8), :] = q[:, k : k + 128]
        out_block[:, x] = wide[...].reshape(C, 8, 128).astype(BF16)
    row = lax.broadcasted_iota(jnp.int32, (C, C), 0)
    col = lax.broadcasted_iota(jnp.int32, (C, C), 1)
    first = proj[0]
    out_proj[0] = jnp.concatenate([first[:, 128:192], first[:, 0:128]], axis=1)
    out_proj[1] = proj[1][:, 0:192]
    for step in range(2):
        out_tri[step] = jnp.where(row >= col, jnp.transpose(tri[step])[0:C], 0.0)


def sum_scratch(size):
    return [pltpu.VMEM((count, size, 128), F32) for count in (32, 31, 16, 32)]


def shards(basis, cell_map, table):
    vmem = pl.BlockSpec(memory_space=pltpu.VMEM)
    hbm = pl.BlockSpec(memory_space=pltpu.MemorySpace.HBM)
    found = pl.pallas_call(
        kernel,
        out_shape=(
            jax.ShapeDtypeStruct((C, 2048), BF16),
            jax.ShapeDtypeStruct((2, C, 256), F32),
            jax.ShapeDtypeStruct((2, C, 128), F32),
        ),
        in_specs=[hbm, hbm, hbm],
        out_specs=(hbm, hbm, hbm),
        scratch_shapes=[
            pltpu.VMEM((C, 2048), BF16),
            pltpu.VMEM((2, C, 256), F32),
            pltpu.VMEM((2, C, 128), F32),
            pltpu.SMEM((8, 27), F32),
            pltpu.VMEM((3, C, 2, 8, 128), BF16),
            pltpu.VMEM((2, 8, 128), jnp.int32),
            pltpu.VMEM((4, 10, 256, 128), BF16),
            pltpu.VMEM((C * 8, 128), F32),
            pltpu.VMEM((16 * 32, 128), F32),
            pltpu.VMEM((16, 3, C, 128), F32),
            pltpu.VMEM((256, 256), F32),
            *sum_scratch(8),
            *sum_scratch(4),
            *sum_scratch(4),
            pltpu.SemaphoreType.DMA((4, 2)),
            pltpu.SemaphoreType.DMA((3, 6)),
            pltpu.SemaphoreType.DMA((3,)),
            pltpu.SemaphoreType.DMA((3,)),
        ],
        compiler_params=pltpu.CompilerParams(
            collective_id=0, has_side_effects=True, vmem_limit_bytes=63 * 1024 * 1024
        ),
    )(table, basis, cell_map)
    block, proj, lower = pl.pallas_call(
        finish,
        out_shape=(
            jax.ShapeDtypeStruct((C, 2, 8, 128), BF16),
            jax.ShapeDtypeStruct((2, C, 192), F32),
            jax.ShapeDtypeStruct((2, C, C), F32),
        ),
        in_specs=[hbm, hbm, hbm],
        out_specs=(vmem, vmem, vmem),
        scratch_shapes=[
            pltpu.VMEM((C, 2048), BF16),
            pltpu.VMEM((2, C, 256), F32),
            pltpu.VMEM((2, C, 128), F32),
            pltpu.VMEM((C * 8, 128), F32),
            pltpu.SemaphoreType.DMA((3,)),
        ],
        compiler_params=pltpu.CompilerParams(vmem_limit_bytes=63 * 1024 * 1024),
    )(*found)
    return block, jnp.swapaxes(proj, 1, 2), lower


def solution(mesh):
    placed = (P(None, None, "slab", "col", None), P("slab", "col", None), P())
    return jax.shard_map(
        shards,
        mesh=mesh,
        in_specs=placed,
        out_specs=(P(None, "slab", "col", None), P(), P()),
        check_vma=False,
    )
```

```python
import functools

import jax
import jax.numpy as jnp
from jax import lax
from jax.experimental import pallas as pl
from jax.experimental.pallas import tpu as pltpu
from jax.sharding import PartitionSpec as P

MESH = pl.DeviceIdType.MESH
F32 = jnp.float32
BF16 = jnp.bfloat16
HIGHEST = lax.Precision.HIGHEST
C = 64
NT = (((1,), (1,)), ((), ()))
NN = (((1,), (0,)), ((), ()))
B1, B2, B0, IM = (pl.ds(i * C, C) for i in range(4))


def fdot(a, b, dims):
    return lax.dot_general(a, b, dims, precision=HIGHEST, preferred_element_type=F32)


def places():
    s = lax.axis_index("slab")
    y = lax.axis_index("col")
    z, r = lax.div(s, 8), lax.rem(s, 8)
    rs = [r] + [lax.rem(r + d, 8) for d in range(1, 8)]
    ys = [y] + [lax.rem(y + d, 4) for d in range(1, 4)]
    zs = [z] + [lax.rem(z + d, 16) for d in range(1, 16)]
    plane = [(z * 8 + a, b) for i, a in enumerate(rs) for j, b in enumerate(ys) if i or j]
    chunk = [a * 4 + b for i, a in enumerate(rs) for j, b in enumerate(ys) if i or j]
    column = [(a * 8 + r, y) for a in zs[1:]]
    sl = [s, lax.rem(s + 1, 128), lax.rem(s + 127, 128)]
    near = [(sl[i], ys[j]) for i in (0, 1, 2) for j in (0, 1, 3) if i or j]
    return s, y, z, r * 4 + y, plane, chunk, column, near


def halo_copies(xe, rows, sems, near):
    x_src = {0: pl.ds(1, 2), 1: pl.ds(2, 1), 2: pl.ds(1, 1)}
    x_dst = {0: pl.ds(1, 2), 1: pl.ds(0, 1), 2: pl.ds(3, 1)}
    y_src = {0: pl.ds(1, 8), 1: pl.ds(8, 1), 3: pl.ds(1, 1)}
    y_dst = {0: pl.ds(1, 8), 1: pl.ds(0, 1), 3: pl.ds(9, 1)}
    out = []
    k = 0
    for i in (0, 1, 2):
        for j in (0, 1, 3):
            if i or j:
                out.append(
                    pltpu.make_async_remote_copy(
                        xe.at[x_src[i], y_src[j], rows],
                        xe.at[x_dst[i], y_dst[j], rows],
                        sems.at[0],
                        sems.at[1],
                        device_id=near[k],
                        device_id_type=MESH,
                    )
                )
                k += 1
    return out


def wait_bytes(ref, sem):
    pltpu.make_async_copy(ref, ref, sem).wait()


class Sum:
    def __init__(self, src, parts, tower, out, sems, place):
        self.src, self.parts, self.tower, self.out, self.sems = src, parts, tower, out, sems
        _, _, self.z, self.mine, self.plane, self.chunk, self.column, _ = place

    def send(self, src, dst, pair, dev):
        pltpu.make_async_remote_copy(
            src, dst, self.sems.at[pair], self.sems.at[pair + 1], device_id=dev, device_id_type=MESH
        ).start()

    def scatter(self):
        for k, dev in enumerate(self.plane):
            self.send(self.src.at[self.chunk[k]], self.parts.at[k], 0, dev)

    def climb(self):
        wait_bytes(self.parts, self.sems.at[1])
        total = self.src[self.mine]
        for k in range(31):
            total = total + self.parts[k]
        self.tower[self.z] = total
        for dev in self.column:
            self.send(self.tower.at[self.z], self.tower.at[self.z], 2, dev)

    def spread(self):
        wait_bytes(self.tower.at[pl.ds(0, 15)], self.sems.at[3])
        total = self.tower[0]
        for k in range(1, 16):
            total = total + self.tower[k]
        self.out[self.mine] = total
        for dev in self.plane:
            self.send(self.out.at[self.mine], self.out.at[self.mine], 4, dev)

    def collect(self):
        wait_bytes(self.out.at[pl.ds(0, 31)], self.sems.at[5])

    def drain(self):
        wait_bytes(self.parts, self.sems.at[0])
        wait_bytes(self.tower.at[pl.ds(0, 15)], self.sems.at[2])
        wait_bytes(self.out.at[pl.ds(0, 31)], self.sems.at[4])


def relayout(basis, xe, wide):
    for b, rows in ((2, B2), (0, B0), (1, B1)):
        for x in range(2):
            wide[...] = basis[b, :, x].astype(F32).reshape(C * 8, 128)
            for y in range(8):
                xe[1 + x, 1 + y, rows, :] = wide[pl.ds(y, C, stride=8), :].astype(BF16)


def coefficients(cell_map, table, coef, s, ycol):
    row = lax.broadcasted_iota(jnp.int32, (8, 128), 0)
    lane = lax.broadcasted_iota(jnp.int32, (8, 128), 1)
    one = jnp.ones((8, 128), F32)
    zero = jnp.zeros((8, 128), F32)
    y_low = jnp.where((row == 0) & (ycol == 0), zero, one)
    y_high = jnp.where((row == 7) & (ycol == 3), zero, one)
    for x in range(2):
        cells = cell_map[x]
        is_class = [cells == k for k in range(8)]
        for o in range(27):
            dx, dy, dz = o // 9, o // 3 % 3, o % 3
            c = zero
            for k in range(8):
                c = jnp.where(is_class[k], table[k, o], c)
            if dx == 0 and x == 0:
                c = jnp.where(s == 0, zero, c)
            if dx == 2 and x == 1:
                c = jnp.where(s == 127, zero, c)
            if dy == 0:
                c = c * y_low
            if dy == 2:
                c = c * y_high
            if dz == 0:
                c = pltpu.roll(jnp.where(lane == 0, zero, c), 127, 1)
            if dz == 2:
                c = pltpu.roll(jnp.where(lane == 127, zero, c), 1, 1)
            coef[pl.ds(x * 8 * 32 + o, 8, stride=32), :] = c


def is_own(x, y):
    return x in (1, 2) and 1 <= y <= 8


def stencil(xe, rows_in, rows_out, coef, held=None, local=None):
    for x in range(2):
        for y in range(8):
            table = coef.at[pl.ds((x * 8 + y) * 32, 32)]
            acc = [None, None, None]
            if local is False:
                acc = [held[x * 8 + y, dz] for dz in range(3)]
            for dx in range(3):
                for dy in range(3):
                    if local is not None and is_own(x + dx, y + dy) != local:
                        continue
                    piece = xe[x + dx, y + dy, rows_in, :].astype(F32)
                    for dz in range(3):
                        o = 9 * dx + 3 * dy + dz
                        term = table[o : o + 1, :] * piece
                        acc[dz] = term if acc[dz] is None else acc[dz] + term
            if local:
                for dz in range(3):
                    held[x * 8 + y, dz] = acc[dz]
            else:
                total = acc[1] + pltpu.roll(acc[0], 1, 1) + pltpu.roll(acc[2], 127, 1)
                xe[x + 1, y + 1, rows_out, :] = total.astype(BF16)


def own_planes(xe, rows):
    return jnp.concatenate([xe[1 + x, 1 + y, rows, :] for x in range(2) for y in range(8)], axis=1)


def gram(left, right):
    return lax.dot_general(left, right, NT, preferred_element_type=F32)


def pack(src, k, v):
    size = src.shape[1]
    for i in range(v.shape[0] // size):
        src[k + i] = v[i * size : (i + 1) * size]


def project(f_full, g):
    col = lax.broadcasted_iota(jnp.int32, (C, 256), 1)
    keep = col < 192
    first = jnp.where(keep, f_full, 0.0)
    first_b = first.astype(BF16).astype(F32)
    second = jnp.where(keep, first - fdot(first_b, g, NN), 0.0)
    second_b = second.astype(BF16).astype(F32)
    rest = jnp.where(keep, second - fdot(second_b, g, NN), 0.0)
    both = first_b + second_b
    pad = jnp.zeros((C, 256), F32)
    lane = lax.broadcasted_iota(jnp.int32, (C, 128), 1)
    own = pltpu.roll(f_full[:, 128:256], 64, 1)
    square = (
        own
        - fdot(first, jnp.concatenate([both, pad], axis=0), NT)
        - fdot(both, jnp.concatenate([rest, pad], axis=0), NT)
    )
    system = jnp.where(lane < C, square, 0.0)
    return first + second, both, rest, system


def splat(v, lane):
    return jnp.broadcast_to(v[:, lane:lane + 1], (8, 128))


def eliminate(m):
    sub = lax.broadcasted_iota(jnp.int32, (8, 128), 0)
    out = [None] * 8
    for j in range(0, 64, 4):
        t, q = j // 8, j % 8
        r = [jnp.broadcast_to(m[t][q + a : q + a + 1, :], (8, 128)) for a in range(4)]
        p = [[splat(r[a], j + b) if b >= a else None for b in range(4)] for a in range(4)]
        det = p[0][0] * p[1][1] - p[0][1] * p[0][1]
        inv = 1.0 / det
        y = [[(p[1][1] * p[0][b] - p[0][1] * p[1][b]) * inv, (p[0][0] * p[1][b] - p[0][1] * p[0][b]) * inv] for b in (2, 3)]
        s22 = p[2][2] - p[0][2] * y[0][0] - p[1][2] * y[0][1]
        s23 = p[2][3] - p[0][2] * y[1][0] - p[1][2] * y[1][1]
        s33 = p[3][3] - p[0][3] * y[1][0] - p[1][3] * y[1][1]
        det2 = s22 * s33 - s23 * s23
        r2 = r[2] - y[0][0] * r[0] - y[0][1] * r[1]
        r3 = r[3] - y[1][0] * r[0] - y[1][1] * r[1]
        if j < 60:
            inv2 = 1.0 / det2
            x0 = (p[1][1] * r[0] - p[0][1] * r[1]) * inv
            x1 = (p[0][0] * r[1] - p[0][1] * r[0]) * inv
            x2 = (s33 * r2 - s23 * r3) * inv2
            x3 = (s22 * r3 - s23 * r2) * inv2
            x0 = x0 - y[0][0] * x2 - y[1][0] * x3
            x1 = x1 - y[0][1] * x2 - y[1][1] * x3
            for v in range(t if q == 0 else t + 1, 8):
                c = [splat(m[v], j + b) for b in range(4)]
                new = m[v] - (c[0] * x0 + c[1] * x1) - (c[2] * x2 + c[3] * x3)
                m[v] = jnp.where(sub >= 4, new, m[v]) if v == t else new
        a0 = lax.rsqrt(p[0][0])
        a1 = lax.rsqrt(det * (1.0 / p[0][0]))
        a2 = lax.rsqrt(s22)
        a3 = lax.rsqrt(det2 * (1.0 / s22))
        u = [r[0] * a0, (r[1] - (p[0][1] * (1.0 / p[0][0])) * r[0]) * a1, r2 * a2, (r3 - (s23 * (1.0 / s22)) * r2) * a3]
        o = out[t] if q else u[3]
        for a in range(4):
            o = jnp.where(sub == q + a, u[a], o)
        out[t] = o
    return out


def factor(system):
    row = lax.broadcasted_iota(jnp.int32, (C, 128), 0)
    lane = lax.broadcasted_iota(jnp.int32, (C, 128), 1)
    diag = jnp.where(lane == row, system, 0.0)
    across = jnp.sum(diag, axis=1, keepdims=True)
    along = jnp.sum(diag, axis=0, keepdims=True)
    scale = lax.rsqrt(across)
    unit = lax.rsqrt(along)
    m = jnp.where(lane < C, system * scale * unit, jnp.where(lane == row + C, scale, 0.0))
    m = jnp.concatenate(eliminate([m[8 * v : 8 * v + 8] for v in range(8)]), axis=0)
    return jnp.where(lane < C, m * (along * unit), m)


def split(v):
    high = v.astype(BF16)
    return high, (v - high.astype(F32)).astype(BF16)


def mixed(weights, v):
    w = lax.dot_general(jnp.concatenate(weights, axis=0), v, NN, preferred_element_type=F32)
    return (w[0:C] + w[C : 2 * C]).astype(BF16)


def kernel(
    table_hbm, basis_hbm, map_hbm,
    w_hbm, proj_hbm, tri_hbm,
    out_w, out_proj, out_tri, table, basis, cell_map, xe, wide, coef, held, gm,
    src0, parts0, tower0, sum0, src1, parts1, tower1, sum1, src2, parts2, tower2, sum2,
    halo_sems, sum_sems, in_sems, out_sems, vouched,
):
    place = places()
    s, ycol, z, p, plane, chunk, column, near = place
    barrier = pltpu.get_barrier_semaphore()
    greeted = plane + near + column[0:4] + column[11:15]
    for dev in greeted:
        pl.semaphore_signal(barrier, inc=1, device_id=dev, device_id_type=MESH)
    loads = [
        pltpu.make_async_copy(basis_hbm, basis, in_sems.at[0]),
        pltpu.make_async_copy(map_hbm, cell_map, in_sems.at[1]),
        pltpu.make_async_copy(table_hbm, table, in_sems.at[2]),
    ]
    for load in loads:
        load.start()
    zero = Sum(src0, parts0, tower0, sum0, sum_sems.at[0], place)
    one = Sum(src1, parts1, tower1, sum1, sum_sems.at[1], place)
    two = Sum(src2, parts2, tower2, sum2, sum_sems.at[2], place)

    loads[0].wait()
    relayout(basis, xe, wide)
    loads[1].wait()
    loads[2].wait()
    coefficients(cell_map, table, coef, s, ycol)
    v = own_planes(xe, pl.ds(0, 192))
    g = gram(v, v[0:128])
    pack(src0, 0, g)
    g = gram(v[128:192], v[128:192])
    pack(src0, 24, jnp.concatenate([g, g], axis=1))

    stencil(xe, B2, IM, coef, held, True)
    pl.semaphore_wait(barrier, len(greeted))
    for copy in halo_copies(xe, B2, halo_sems.at[0], near):
        copy.start()
    zero.scatter()
    for dev in (column[3], column[11]):
        pl.semaphore_signal(vouched, inc=1, device_id=dev, device_id_type=MESH)
    moved = xe.at[pl.ds(0, 3), pl.ds(0, 8), B2]
    wait_bytes(moved, halo_sems.at[0, 1])
    stencil(xe, B2, IM, coef, held, False)

    x = own_planes(xe, pl.ds(0, 256))
    f = gram(x[192:256], x)
    pack(src1, 0, f[:, 0:128])
    pack(src1, 16, f[:, 128:256])
    one.scatter()
    pl.semaphore_wait(vouched, 2)
    zero.climb()
    for k, rows in ((1, B0), (2, B1), (3, IM)):
        for copy in halo_copies(xe, rows, halo_sems.at[k], near):
            copy.start()
    one.climb()
    zero.spread()
    one.spread()
    zero.collect()
    one.collect()

    scale = 1.0 / (256 * 32 * 128)
    gm[0:192, 0:128] = sum0[0:24].reshape(192, 128) * scale
    gm[0:128, 128:192] = jnp.transpose(gm[128:192, 0:128])
    gm[0:192, 192:256] = jnp.zeros((192, 64), F32)
    gm[192:256, :] = jnp.zeros((64, 256), F32)
    gm[128:192, 128:192] = sum0[24:32].reshape(64, 128)[:, 0:64] * scale
    f = jnp.concatenate([sum1[0:16].reshape(64, 128), sum1[16:32].reshape(64, 128)], axis=1) * scale
    proj, both, rest, system = project(f, gm[...])
    out_proj[0] = proj

    col = lax.broadcasted_iota(jnp.int32, (C, 256), 1)
    row = lax.broadcasted_iota(jnp.int32, (C, 256), 0)
    weights = split(jnp.where(col == row + 192, 1.0, -both))
    for k in range(4):
        wait_bytes(moved, halo_sems.at[k, 0])
        if k:
            wait_bytes(moved, halo_sems.at[k, 1])

    def correct(x, carry):
        v = jnp.concatenate([xe[x, y] for y in range(10)], axis=1)
        w = mixed(weights, v)
        for y in range(10):
            xe[x, y, B0, :] = w[:, y * 128 : (y + 1) * 128]
        return carry

    lax.fori_loop(0, 4, correct, 0)
    stencil(xe, B0, IM, coef)

    x = own_planes(xe, pl.ds(0, 256))
    h = gram(x[192:256], x)
    pack(src2, 0, h[:, 0:128])
    pack(src2, 16, h[:, 128:256])
    two.scatter()
    two.climb()

    done = factor(system)
    out_tri[0] = done
    inverse = pltpu.roll(done, 64, 1)[:, 0:C].astype(BF16).astype(F32)
    none = jnp.zeros((C, C), F32)
    q_left = fdot(inverse, rest[:, 0:128], NN)
    q_own = fdot(fdot(inverse, system[:, 0:C], NN), inverse, NT)
    gm[128:192, 0:128] = q_left
    gm[0:128, 128:192] = jnp.transpose(q_left)
    gm[128:192, 128:192] = q_own
    twice = jnp.concatenate(
        [jnp.concatenate([inverse, none], axis=1), jnp.concatenate([none, inverse], axis=1)], axis=0
    )

    two.spread()
    two.collect()
    h = jnp.concatenate([sum2[0:16].reshape(64, 128), sum2[16:32].reshape(64, 128)], axis=1) * scale
    h = fdot(inverse, h, NN)
    f = jnp.concatenate([h[:, 0:128], fdot(h[:, 128:256], twice, NT)], axis=1)
    proj, both, rest, system = project(f, gm[...])
    out_proj[1] = proj
    lane = lax.broadcasted_iota(jnp.int32, (C, 128), 1)
    unit = lax.broadcasted_iota(jnp.int32, (C, 128), 0) + C
    right = fdot(jnp.where(lane < C, -both[:, 128:256], jnp.where(lane == unit, 1.0, 0.0)), twice, NN)
    weights = split(jnp.concatenate([-both[:, 0:128], right], axis=1))
    out_w[...] = mixed(weights, own_planes(xe, pl.ds(0, 256)))
    stores = [
        pltpu.make_async_copy(out_proj, proj_hbm, out_sems.at[0]),
        pltpu.make_async_copy(out_w, w_hbm, out_sems.at[1]),
        pltpu.make_async_copy(out_tri, tri_hbm, out_sems.at[2]),
    ]
    stores[0].start()
    stores[1].start()
    out_tri[1] = factor(system)
    stores[2].start()
    zero.drain()
    one.drain()
    two.drain()
    for store in stores:
        store.wait()


def finish(w_hbm, proj_hbm, tri_hbm, out_block, out_proj, out_tri, w, proj, tri, wide, sems):
    loads = [
        pltpu.make_async_copy(tri_hbm, tri, sems.at[0]),
        pltpu.make_async_copy(w_hbm, w, sems.at[1]),
        pltpu.make_async_copy(proj_hbm, proj, sems.at[2]),
    ]
    for load in loads:
        load.start()
    for load in loads:
        load.wait()
    inverse = pltpu.roll(tri[1], 64, 1)[:, 0:C].astype(BF16)
    q = lax.dot_general(inverse, w[...], NN, preferred_element_type=F32)
    for x in range(2):
        for y in range(8):
            k = (x * 8 + y) * 128
            wide[pl.ds(y, C, stride=8), :] = q[:, k : k + 128]
        out_block[:, x] = wide[...].reshape(C, 8, 128).astype(BF16)
    row = lax.broadcasted_iota(jnp.int32, (C, C), 0)
    col = lax.broadcasted_iota(jnp.int32, (C, C), 1)
    first = proj[0]
    out_proj[0] = jnp.concatenate([first[:, 128:192], first[:, 0:128]], axis=1)
    out_proj[1] = proj[1][:, 0:192]
    for step in range(2):
        out_tri[step] = jnp.where(row >= col, jnp.transpose(tri[step])[0:C], 0.0)


def sum_scratch(size):
    return [pltpu.VMEM((count, size, 128), F32) for count in (32, 31, 16, 32)]


def shards(basis, cell_map, table):
    vmem = pl.BlockSpec(memory_space=pltpu.VMEM)
    hbm = pl.BlockSpec(memory_space=pltpu.MemorySpace.HBM)
    found = pl.pallas_call(
        kernel,
        out_shape=(
            jax.ShapeDtypeStruct((C, 2048), BF16),
            jax.ShapeDtypeStruct((2, C, 256), F32),
            jax.ShapeDtypeStruct((2, C, 128), F32),
        ),
        in_specs=[hbm, hbm, hbm],
        out_specs=(hbm, hbm, hbm),
        scratch_shapes=[
            pltpu.VMEM((C, 2048), BF16),
            pltpu.VMEM((2, C, 256), F32),
            pltpu.VMEM((2, C, 128), F32),
            pltpu.SMEM((8, 27), F32),
            pltpu.VMEM((3, C, 2, 8, 128), BF16),
            pltpu.VMEM((2, 8, 128), jnp.int32),
            pltpu.VMEM((4, 10, 256, 128), BF16),
            pltpu.VMEM((C * 8, 128), F32),
            pltpu.VMEM((16 * 32, 128), F32),
            pltpu.VMEM((16, 3, C, 128), F32),
            pltpu.VMEM((256, 256), F32),
            *sum_scratch(8),
            *sum_scratch(4),
            *sum_scratch(4),
            pltpu.SemaphoreType.DMA((4, 2)),
            pltpu.SemaphoreType.DMA((3, 6)),
            pltpu.SemaphoreType.DMA((3,)),
            pltpu.SemaphoreType.DMA((3,)),
            pltpu.SemaphoreType.REGULAR,
        ],
        compiler_params=pltpu.CompilerParams(
            collective_id=0, has_side_effects=True, vmem_limit_bytes=63 * 1024 * 1024
        ),
    )(table, basis, cell_map)
    block, proj, lower = pl.pallas_call(
        finish,
        out_shape=(
            jax.ShapeDtypeStruct((C, 2, 8, 128), BF16),
            jax.ShapeDtypeStruct((2, C, 192), F32),
            jax.ShapeDtypeStruct((2, C, C), F32),
        ),
        in_specs=[hbm, hbm, hbm],
        out_specs=(vmem, vmem, vmem),
        scratch_shapes=[
            pltpu.VMEM((C, 2048), BF16),
            pltpu.VMEM((2, C, 256), F32),
            pltpu.VMEM((2, C, 128), F32),
            pltpu.VMEM((C * 8, 128), F32),
            pltpu.SemaphoreType.DMA((3,)),
        ],
        compiler_params=pltpu.CompilerParams(vmem_limit_bytes=63 * 1024 * 1024),
    )(*found)
    return block, jnp.swapaxes(proj, 1, 2), lower


def solution(mesh):
    placed = (P(None, None, "slab", "col", None), P("slab", "col", None), P())
    return jax.shard_map(
        shards,
        mesh=mesh,
        in_specs=placed,
        out_specs=(P(None, "slab", "col", None), P(), P()),
        check_vma=False,
    )
```

```python
import functools

import jax
import jax.numpy as jnp
from jax import lax
from jax.experimental import pallas as pl
from jax.experimental.pallas import tpu as pltpu
from jax.sharding import PartitionSpec as P

MESH = pl.DeviceIdType.MESH
F32 = jnp.float32
BF16 = jnp.bfloat16
HIGHEST = lax.Precision.HIGHEST
C = 64
NT = (((1,), (1,)), ((), ()))
NN = (((1,), (0,)), ((), ()))
B1, B2, B0, IM = (pl.ds(i * C, C) for i in range(4))


def fdot(a, b, dims):
    return lax.dot_general(a, b, dims, precision=HIGHEST, preferred_element_type=F32)


def places():
    s = lax.axis_index("slab")
    y = lax.axis_index("col")
    z, r = lax.div(s, 8), lax.rem(s, 8)
    x, core = lax.div(r, 2), lax.rem(r, 2)
    xs = [x] + [lax.rem(x + d, 4) for d in range(1, 4)]
    ys = [y] + [lax.rem(y + d, 4) for d in range(1, 4)]
    zs = [z] + [lax.rem(z + d, 16) for d in range(1, 16)]
    cores = [core, 1 - core]
    steps = [(i, j, k) for i in range(4) for j in range(4) for k in range(2) if i or j or k]
    steps.sort(key=lambda t: -(min(t[0], 4 - t[0]) + min(t[1], 4 - t[1]) + t[2] * 0.3))
    plane = [(z * 8 + xs[i] * 2 + cores[k], ys[j]) for i, j, k in steps]
    chunk = [(xs[i] * 2 + cores[k]) * 4 + ys[j] for i, j, k in steps]
    column = {d: (zs[d] * 8 + r, y) for d in sorted(range(1, 16), key=lambda d: -min(d, 16 - d))}
    sl = [s, lax.rem(s + 1, 128), lax.rem(s + 127, 128)]
    near = [(sl[i], ys[j]) for i in (0, 1, 2) for j in (0, 1, 3) if i or j]
    return s, y, z, r * 4 + y, plane, chunk, column, near


def halo_copies(xe, rows, sems, near):
    x_src = {0: pl.ds(1, 2), 1: pl.ds(2, 1), 2: pl.ds(1, 1)}
    x_dst = {0: pl.ds(1, 2), 1: pl.ds(0, 1), 2: pl.ds(3, 1)}
    y_src = {0: pl.ds(1, 8), 1: pl.ds(8, 1), 3: pl.ds(1, 1)}
    y_dst = {0: pl.ds(1, 8), 1: pl.ds(0, 1), 3: pl.ds(9, 1)}
    out = []
    k = 0
    for i in (0, 1, 2):
        for j in (0, 1, 3):
            if i or j:
                out.append(
                    pltpu.make_async_remote_copy(
                        xe.at[x_src[i], y_src[j], rows],
                        xe.at[x_dst[i], y_dst[j], rows],
                        sems.at[0],
                        sems.at[1],
                        device_id=near[k],
                        device_id_type=MESH,
                    )
                )
                k += 1
    return out


def wait_bytes(ref, sem):
    pltpu.make_async_copy(ref, ref, sem).wait()


class Sum:
    def __init__(self, src, parts, tower, out, sems, place):
        self.src, self.parts, self.tower, self.out, self.sems = src, parts, tower, out, sems
        _, _, self.z, self.mine, self.plane, self.chunk, self.column, _ = place

    def send(self, src, dst, pair, dev):
        pltpu.make_async_remote_copy(
            src, dst, self.sems.at[pair], self.sems.at[pair + 1], device_id=dev, device_id_type=MESH
        ).start()

    def scatter(self):
        for k, dev in enumerate(self.plane):
            self.send(self.src.at[self.chunk[k]], self.parts.at[k], 0, dev)

    def climb(self, change=None):
        wait_bytes(self.parts, self.sems.at[1])
        total = self.src[self.mine]
        for k in range(31):
            total = total + self.parts[k]
        self.tower[self.z] = total if change is None else change(total)
        for dev in self.column.values():
            self.send(self.tower.at[self.z], self.tower.at[self.z], 2, dev)

    def spread(self):
        wait_bytes(self.tower.at[pl.ds(0, 15)], self.sems.at[3])
        total = self.tower[0]
        for k in range(1, 16):
            total = total + self.tower[k]
        self.out[self.mine] = total
        for dev in self.plane:
            self.send(self.out.at[self.mine], self.out.at[self.mine], 4, dev)

    def collect(self):
        wait_bytes(self.out.at[pl.ds(0, 31)], self.sems.at[5])

    def drain(self):
        wait_bytes(self.parts, self.sems.at[0])
        wait_bytes(self.tower.at[pl.ds(0, 15)], self.sems.at[2])
        wait_bytes(self.out.at[pl.ds(0, 31)], self.sems.at[4])


def relayout(basis, xe, wide):
    for b, rows in ((2, B2), (0, B0), (1, B1)):
        for x in range(2):
            wide[...] = basis[b, :, x].astype(F32).reshape(C * 8, 128)
            for y in range(8):
                xe[1 + x, 1 + y, rows, :] = wide[pl.ds(y, C, stride=8), :].astype(BF16)


def coefficients(cell_map, table, coef, s, ycol):
    row = lax.broadcasted_iota(jnp.int32, (8, 128), 0)
    lane = lax.broadcasted_iota(jnp.int32, (8, 128), 1)
    one = jnp.ones((8, 128), F32)
    zero = jnp.zeros((8, 128), F32)
    y_low = jnp.where((row == 0) & (ycol == 0), zero, one)
    y_high = jnp.where((row == 7) & (ycol == 3), zero, one)
    for x in range(2):
        cells = cell_map[x]
        is_class = [cells == k for k in range(8)]
        for o in range(27):
            dx, dy, dz = o // 9, o // 3 % 3, o % 3
            c = zero
            for k in range(8):
                c = jnp.where(is_class[k], table[k, o], c)
            if dx == 0 and x == 0:
                c = jnp.where(s == 0, zero, c)
            if dx == 2 and x == 1:
                c = jnp.where(s == 127, zero, c)
            if dy == 0:
                c = c * y_low
            if dy == 2:
                c = c * y_high
            if dz == 0:
                c = pltpu.roll(jnp.where(lane == 0, zero, c), 127, 1)
            if dz == 2:
                c = pltpu.roll(jnp.where(lane == 127, zero, c), 1, 1)
            coef[pl.ds(x * 8 * 32 + o, 8, stride=32), :] = c


def is_own(x, y):
    return x in (1, 2) and 1 <= y <= 8


def total_of(acc):
    return (acc[1] + pltpu.roll(acc[0], 1, 1) + pltpu.roll(acc[2], 127, 1)).astype(BF16)


def split_stencil(xe, rows, coef, held, local, put):
    for x in range(2):
        for y in range(8):
            table = coef.at[pl.ds((x * 8 + y) * 32, 32)]
            acc = [None, None, None] if local else [held[x * 8 + y, dz] for dz in range(3)]
            for dx in range(3):
                for dy in range(3):
                    if is_own(x + dx, y + dy) != local:
                        continue
                    piece = xe[x + dx, y + dy, rows, :].astype(F32)
                    for dz in range(3):
                        o = 9 * dx + 3 * dy + dz
                        term = table[o : o + 1, :] * piece
                        acc[dz] = term if acc[dz] is None else acc[dz] + term
            if local:
                for dz in range(3):
                    held[x * 8 + y, dz] = acc[dz]
            else:
                put(x, y, total_of(acc))


def stencil(xe, rows, coef, put):
    for x in range(2):

        def body(y, carry):
            table = coef.at[pl.ds(pl.multiple_of((x * 8 + y) * 32, 32), 32)]
            acc = [jnp.zeros((C, 128), F32) for _ in range(3)]
            for dx in range(3):
                for dy in range(3):
                    piece = xe[x + dx, y + dy, rows, :].astype(F32)
                    for dz in range(3):
                        o = 9 * dx + 3 * dy + dz
                        acc[dz] = acc[dz] + table[o : o + 1, :] * piece
            put(x, y, total_of(acc))
            return carry

        lax.fori_loop(0, 8, body, 0)


def own_planes(xe, rows):
    return jnp.concatenate([xe[1 + x, 1 + y, rows, :] for x in range(2) for y in range(8)], axis=1)


def gram(left, right):
    return lax.dot_general(left, right, NT, preferred_element_type=F32)


def pack(src, k, v):
    size = src.shape[1]
    for i in range(v.shape[0] // size):
        src[k + i] = v[i * size : (i + 1) * size]


def project(f_full, g):
    col = lax.broadcasted_iota(jnp.int32, (C, 256), 1)
    keep = col < 192
    first = jnp.where(keep, f_full, 0.0)
    first_b = first.astype(BF16).astype(F32)
    second = jnp.where(keep, first - fdot(first_b, g, NN), 0.0)
    second_b = second.astype(BF16).astype(F32)
    rest = jnp.where(keep, second - fdot(second_b, g, NN), 0.0)
    both = first_b + second_b
    pad = jnp.zeros((C, 256), F32)
    lane = lax.broadcasted_iota(jnp.int32, (C, 128), 1)
    own = pltpu.roll(f_full[:, 128:256], 64, 1)
    square = (
        own
        - fdot(first, jnp.concatenate([both, pad], axis=0), NT)
        - fdot(both, jnp.concatenate([rest, pad], axis=0), NT)
    )
    system = jnp.where(lane < C, square, 0.0)
    return first + second, both, rest, system


def splat(v, lane):
    return jnp.broadcast_to(v[:, lane:lane + 1], (8, 128))


def eliminate(m):
    sub = lax.broadcasted_iota(jnp.int32, (8, 128), 0)
    out = [None] * 8
    for j in range(0, 64, 4):
        t, q = j // 8, j % 8
        r = [jnp.broadcast_to(m[t][q + a : q + a + 1, :], (8, 128)) for a in range(4)]
        p = [[splat(r[a], j + b) if b >= a else None for b in range(4)] for a in range(4)]
        det = p[0][0] * p[1][1] - p[0][1] * p[0][1]
        inv = 1.0 / det
        y = [[(p[1][1] * p[0][b] - p[0][1] * p[1][b]) * inv, (p[0][0] * p[1][b] - p[0][1] * p[0][b]) * inv] for b in (2, 3)]
        s22 = p[2][2] - p[0][2] * y[0][0] - p[1][2] * y[0][1]
        s23 = p[2][3] - p[0][2] * y[1][0] - p[1][2] * y[1][1]
        s33 = p[3][3] - p[0][3] * y[1][0] - p[1][3] * y[1][1]
        det2 = s22 * s33 - s23 * s23
        r2 = r[2] - y[0][0] * r[0] - y[0][1] * r[1]
        r3 = r[3] - y[1][0] * r[0] - y[1][1] * r[1]
        if j < 60:
            inv2 = 1.0 / det2
            x0 = (p[1][1] * r[0] - p[0][1] * r[1]) * inv
            x1 = (p[0][0] * r[1] - p[0][1] * r[0]) * inv
            x2 = (s33 * r2 - s23 * r3) * inv2
            x3 = (s22 * r3 - s23 * r2) * inv2
            x0 = x0 - y[0][0] * x2 - y[1][0] * x3
            x1 = x1 - y[0][1] * x2 - y[1][1] * x3
            for v in range(t if q == 0 else t + 1, 8):
                c = [splat(m[v], j + b) for b in range(4)]
                new = m[v] - (c[0] * x0 + c[1] * x1) - (c[2] * x2 + c[3] * x3)
                m[v] = jnp.where(sub >= 4, new, m[v]) if v == t else new
        a0 = lax.rsqrt(p[0][0])
        a1 = lax.rsqrt(det * (1.0 / p[0][0]))
        a2 = lax.rsqrt(s22)
        a3 = lax.rsqrt(det2 * (1.0 / s22))
        u = [r[0] * a0, (r[1] - (p[0][1] * (1.0 / p[0][0])) * r[0]) * a1, r2 * a2, (r3 - (s23 * (1.0 / s22)) * r2) * a3]
        o = out[t] if q else u[3]
        for a in range(4):
            o = jnp.where(sub == q + a, u[a], o)
        out[t] = o
    return out


def factor(system):
    row = lax.broadcasted_iota(jnp.int32, (C, 128), 0)
    lane = lax.broadcasted_iota(jnp.int32, (C, 128), 1)
    diag = jnp.where(lane == row, system, 0.0)
    across = jnp.sum(diag, axis=1, keepdims=True)
    along = jnp.sum(diag, axis=0, keepdims=True)
    scale = lax.rsqrt(across)
    unit = lax.rsqrt(along)
    m = jnp.where(lane < C, system * scale * unit, jnp.where(lane == row + C, scale, 0.0))
    m = jnp.concatenate(eliminate([m[8 * v : 8 * v + 8] for v in range(8)]), axis=0)
    return jnp.where(lane < C, m * (along * unit), m)


def split(v):
    high = v.astype(BF16)
    return high, (v - high.astype(F32)).astype(BF16)


def mixed(weights, v):
    w = lax.dot_general(jnp.concatenate(weights, axis=0), v, NN, preferred_element_type=F32)
    return (w[0:C] + w[C : 2 * C]).astype(BF16)


def kernel(
    table_hbm, basis_hbm, map_hbm,
    w_hbm, proj_hbm, tri_hbm,
    out_w, out_proj, out_tri, table, basis, cell_map, xe, wide, coef, held, image, gm,
    src0, parts0, tower0, sum0, src1, parts1, tower1, sum1, src2, parts2, tower2, sum2,
    halo_sems, sum_sems, in_sems, out_sems, vouched,
):
    place = places()
    s, ycol, z, p, plane, chunk, column, near = place
    barrier = pltpu.get_barrier_semaphore()
    greeted = [column[d] for d in (4, 12, 3, 13, 2, 14, 1, 15)] + plane + near
    for dev in greeted:
        pl.semaphore_signal(barrier, inc=1, device_id=dev, device_id_type=MESH)
    loads = [
        pltpu.make_async_copy(basis_hbm, basis, in_sems.at[0]),
        pltpu.make_async_copy(map_hbm, cell_map, in_sems.at[1]),
        pltpu.make_async_copy(table_hbm, table, in_sems.at[2]),
    ]
    for load in loads:
        load.start()
    zero = Sum(src0, parts0, tower0, sum0, sum_sems.at[0], place)
    one = Sum(src1, parts1, tower1, sum1, sum_sems.at[1], place)
    two = Sum(src2, parts2, tower2, sum2, sum_sems.at[2], place)

    loads[0].wait()
    relayout(basis, xe, wide)
    loads[1].wait()
    loads[2].wait()
    coefficients(cell_map, table, coef, s, ycol)
    v = own_planes(xe, pl.ds(0, 192))
    g = gram(v, v[0:128])
    pack(src0, 0, g)
    g = gram(v[128:192], v[128:192])
    pack(src0, 24, jnp.concatenate([g, g], axis=1))

    split_stencil(xe, B2, coef, held, True, None)
    pl.semaphore_wait(barrier, len(greeted))
    for copy in halo_copies(xe, B2, halo_sems.at[0], near):
        copy.start()
    zero.scatter()
    for dev in (column[4], column[12]):
        pl.semaphore_signal(vouched, inc=1, device_id=dev, device_id_type=MESH)
    for k, rows in ((1, B1), (2, B0)):
        for copy in halo_copies(xe, rows, halo_sems.at[k], near):
            copy.start()
    moved = xe.at[pl.ds(0, 3), pl.ds(0, 8), B2]

    def put_w(x, y, v):
        xe[x + 1, y + 1, IM, :] = v
        image[x * 8 + y, C : 2 * C, :] = v

    def put_at(k):
        def put(x, y, v):
            image[x * 8 + y, k * C : (k + 1) * C, :] = v

        return put

    wait_bytes(moved, halo_sems.at[0, 1])
    split_stencil(xe, B2, coef, held, False, put_w)

    x = own_planes(xe, pl.ds(0, 256))
    f = gram(x[192:256], x)
    pack(src1, 0, f[:, 0:128])
    pack(src1, 16, f[:, 128:256])
    one.scatter()
    pl.semaphore_wait(vouched, 2)
    zero.climb()
    for copy in halo_copies(xe, IM, halo_sems.at[3], near):
        copy.start()
    wait_bytes(moved, halo_sems.at[1, 1])
    stencil(xe, B1, coef, put_at(0))
    one.climb()
    wait_bytes(moved, halo_sems.at[2, 1])
    stencil(xe, B0, coef, put_at(2))
    zero.spread()
    wait_bytes(moved, halo_sems.at[3, 1])
    stencil(xe, IM, coef, put_at(3))
    x = own_planes(xe, pl.ds(0, 256))
    y = jnp.concatenate([image[k] for k in range(16)], axis=1)
    for i, left in enumerate((x, y)):
        g = gram(left, y)
        for k in range(32):
            for half in range(2):
                at = 16 * i + 8 * half
                src2[k, at : at + 8, :] = g[8 * k : 8 * k + 8, 128 * half : 128 * half + 128]
    one.spread()
    two.scatter()
    zero.collect()
    one.collect()

    scale = 1.0 / (256 * 32 * 128)
    gm[0:192, 0:128] = sum0[0:24].reshape(192, 128) * scale
    gm[0:128, 128:192] = jnp.transpose(gm[128:192, 0:128])
    gm[0:192, 192:256] = jnp.zeros((192, 64), F32)
    gm[192:256, :] = jnp.zeros((64, 256), F32)
    gm[128:192, 128:192] = sum0[24:32].reshape(64, 128)[:, 0:64] * scale
    f = jnp.concatenate([sum1[0:16].reshape(64, 128), sum1[16:32].reshape(64, 128)], axis=1) * scale
    proj, both, rest, system = project(f, gm[...])
    out_proj[0] = proj

    col = lax.broadcasted_iota(jnp.int32, (C, 256), 1)
    row = lax.broadcasted_iota(jnp.int32, (C, 256), 0)
    mix = jnp.where(col == row + 192, 1.0, -both)
    empty = jnp.zeros((C, 256), F32)
    mix_both = jnp.concatenate(
        [jnp.concatenate([mix, empty], axis=1), jnp.concatenate([empty, mix], axis=1)], axis=0
    )

    def contract(total):
        wide_row = jnp.concatenate([total[8 * k : 8 * k + 8] for k in range(4)], axis=1)
        return fdot(wide_row, mix_both, NT)

    two.climb(contract)

    for k in range(4):
        wait_bytes(moved, halo_sems.at[k, 0])
    weights = split(mix)
    x = own_planes(xe, pl.ds(0, 256))
    y = jnp.concatenate([image[k] for k in range(16)], axis=1)
    for rows, v in ((B0, mixed(weights, x)), (IM, mixed(weights, y))):
        for k in range(16):
            xe[1 + k // 8, 1 + k % 8, rows, :] = v[:, 128 * k : 128 * k + 128]

    done = factor(system)
    out_tri[0] = done
    inverse = pltpu.roll(done, 64, 1)[:, 0:C].astype(BF16).astype(F32)
    none = jnp.zeros((C, C), F32)
    q_left = fdot(inverse, rest[:, 0:128], NN)
    q_own = fdot(fdot(inverse, system[:, 0:C], NN), inverse, NT)
    gm[128:192, 0:128] = q_left
    gm[0:128, 128:192] = jnp.transpose(q_left)
    gm[128:192, 128:192] = q_own
    twice = jnp.concatenate(
        [jnp.concatenate([inverse, none], axis=1), jnp.concatenate([none, inverse], axis=1)], axis=0
    )

    two.spread()
    two.collect()
    h = sum2[...].reshape(256, 128) * scale
    own = fdot(mix, h, NN)
    h = jnp.concatenate([h[0:128, 0:C], own[:, 0:C], pltpu.roll(own, 64, 1)[:, 0:C]], axis=0)
    h = fdot(inverse, h, NT)
    f = jnp.concatenate([h[:, 0:128], fdot(h[:, 128:256], twice, NT)], axis=1)
    proj, both, rest, system = project(f, gm[...])
    out_proj[1] = proj
    lane = lax.broadcasted_iota(jnp.int32, (C, 128), 1)
    unit = lax.broadcasted_iota(jnp.int32, (C, 128), 0) + C
    right = fdot(jnp.where(lane < C, -both[:, 128:256], jnp.where(lane == unit, 1.0, 0.0)), twice, NN)
    weights = split(jnp.concatenate([-both[:, 0:128], right], axis=1))
    out_w[...] = mixed(weights, own_planes(xe, pl.ds(0, 256)))
    stores = [
        pltpu.make_async_copy(out_proj, proj_hbm, out_sems.at[0]),
        pltpu.make_async_copy(out_w, w_hbm, out_sems.at[1]),
        pltpu.make_async_copy(out_tri, tri_hbm, out_sems.at[2]),
    ]
    stores[0].start()
    stores[1].start()
    out_tri[1] = factor(system)
    stores[2].start()
    zero.drain()
    one.drain()
    two.drain()
    for store in stores:
        store.wait()


def finish(w_hbm, proj_hbm, tri_hbm, out_block, out_proj, out_tri, w, proj, tri, wide, sems):
    loads = [
        pltpu.make_async_copy(tri_hbm, tri, sems.at[0]),
        pltpu.make_async_copy(w_hbm, w, sems.at[1]),
        pltpu.make_async_copy(proj_hbm, proj, sems.at[2]),
    ]
    for load in loads:
        load.start()
    for load in loads:
        load.wait()
    inverse = pltpu.roll(tri[1], 64, 1)[:, 0:C].astype(BF16)
    q = lax.dot_general(inverse, w[...], NN, preferred_element_type=F32)
    for x in range(2):
        for y in range(8):
            k = (x * 8 + y) * 128
            wide[pl.ds(y, C, stride=8), :] = q[:, k : k + 128]
        out_block[:, x] = wide[...].reshape(C, 8, 128).astype(BF16)
    row = lax.broadcasted_iota(jnp.int32, (C, C), 0)
    col = lax.broadcasted_iota(jnp.int32, (C, C), 1)
    first = proj[0]
    out_proj[0] = jnp.concatenate([first[:, 128:192], first[:, 0:128]], axis=1)
    out_proj[1] = proj[1][:, 0:192]
    for step in range(2):
        out_tri[step] = jnp.where(row >= col, jnp.transpose(tri[step])[0:C], 0.0)


def sum_scratch(sent, kept):
    return [pltpu.VMEM((count, size, 128), F32) for count, size in ((32, sent), (31, sent), (16, kept), (32, kept))]


def shards(basis, cell_map, table):
    vmem = pl.BlockSpec(memory_space=pltpu.VMEM)
    hbm = pl.BlockSpec(memory_space=pltpu.MemorySpace.HBM)
    found = pl.pallas_call(
        kernel,
        out_shape=(
            jax.ShapeDtypeStruct((C, 2048), BF16),
            jax.ShapeDtypeStruct((2, C, 256), F32),
            jax.ShapeDtypeStruct((2, C, 128), F32),
        ),
        in_specs=[hbm, hbm, hbm],
        out_specs=(hbm, hbm, hbm),
        scratch_shapes=[
            pltpu.VMEM((C, 2048), BF16),
            pltpu.VMEM((2, C, 256), F32),
            pltpu.VMEM((2, C, 128), F32),
            pltpu.SMEM((8, 27), F32),
            pltpu.VMEM((3, C, 2, 8, 128), BF16),
            pltpu.VMEM((2, 8, 128), jnp.int32),
            pltpu.VMEM((4, 10, 256, 128), BF16),
            pltpu.VMEM((C * 8, 128), F32),
            pltpu.VMEM((16 * 32, 128), F32),
            pltpu.VMEM((16, 3, C, 128), F32),
            pltpu.VMEM((16, 256, 128), BF16),
            pltpu.VMEM((256, 256), F32),
            *sum_scratch(8, 8),
            *sum_scratch(4, 4),
            *sum_scratch(32, 8),
            pltpu.SemaphoreType.DMA((4, 2)),
            pltpu.SemaphoreType.DMA((3, 6)),
            pltpu.SemaphoreType.DMA((3,)),
            pltpu.SemaphoreType.DMA((3,)),
            pltpu.SemaphoreType.REGULAR,
        ],
        compiler_params=pltpu.CompilerParams(
            collective_id=0, has_side_effects=True, vmem_limit_bytes=63 * 1024 * 1024
        ),
    )(table, basis, cell_map)
    block, proj, lower = pl.pallas_call(
        finish,
        out_shape=(
            jax.ShapeDtypeStruct((C, 2, 8, 128), BF16),
            jax.ShapeDtypeStruct((2, C, 192), F32),
            jax.ShapeDtypeStruct((2, C, C), F32),
        ),
        in_specs=[hbm, hbm, hbm],
        out_specs=(vmem, vmem, vmem),
        scratch_shapes=[
            pltpu.VMEM((C, 2048), BF16),
            pltpu.VMEM((2, C, 256), F32),
            pltpu.VMEM((2, C, 128), F32),
            pltpu.VMEM((C * 8, 128), F32),
            pltpu.SemaphoreType.DMA((3,)),
        ],
        compiler_params=pltpu.CompilerParams(vmem_limit_bytes=63 * 1024 * 1024),
    )(*found)
    return block, jnp.swapaxes(proj, 1, 2), lower


def solution(mesh):
    placed = (P(None, None, "slab", "col", None), P("slab", "col", None), P())
    return jax.shard_map(
        shards,
        mesh=mesh,
        in_specs=placed,
        out_specs=(P(None, "slab", "col", None), P(), P()),
        check_vma=False,
    )
```

```python
import functools

import jax
import jax.numpy as jnp
from jax import lax
from jax.experimental import pallas as pl
from jax.experimental.pallas import tpu as pltpu
from jax.sharding import PartitionSpec as P

MESH = pl.DeviceIdType.MESH
F32 = jnp.float32
BF16 = jnp.bfloat16
HIGHEST = lax.Precision.HIGHEST
C = 64
NT = (((1,), (1,)), ((), ()))
NN = (((1,), (0,)), ((), ()))
B1, B2, B0, IM = (pl.ds(i * C, C) for i in range(4))


def fdot(a, b, dims):
    return lax.dot_general(a, b, dims, precision=HIGHEST, preferred_element_type=F32)


def places():
    s = lax.axis_index("slab")
    y = lax.axis_index("col")
    z, r = lax.div(s, 8), lax.rem(s, 8)
    x, core = lax.div(r, 2), lax.rem(r, 2)
    xs = [x] + [lax.rem(x + d, 4) for d in range(1, 4)]
    ys = [y] + [lax.rem(y + d, 4) for d in range(1, 4)]
    zs = [z] + [lax.rem(z + d, 16) for d in range(1, 16)]
    cores = [core, 1 - core]
    steps = [(i, j, k) for i in range(4) for j in range(4) for k in range(2) if i or j or k]
    steps.sort(key=lambda t: -(min(t[0], 4 - t[0]) + min(t[1], 4 - t[1]) + t[2] * 0.3))
    plane = [(z * 8 + xs[i] * 2 + cores[k], ys[j]) for i, j, k in steps]
    chunk = [(xs[i] * 2 + cores[k]) * 4 + ys[j] for i, j, k in steps]
    column = {d: (zs[d] * 8 + r, y) for d in sorted(range(1, 16), key=lambda d: -min(d, 16 - d))}
    sl = [s, lax.rem(s + 1, 128), lax.rem(s + 127, 128)]
    near = [(sl[i], ys[j]) for i in (0, 1, 2) for j in (0, 1, 3) if i or j]
    return s, y, z, r * 4 + y, plane, chunk, column, near


def halo_copies(xe, rows, sems, near):
    x_src = {0: pl.ds(1, 2), 1: pl.ds(2, 1), 2: pl.ds(1, 1)}
    x_dst = {0: pl.ds(1, 2), 1: pl.ds(0, 1), 2: pl.ds(3, 1)}
    y_src = {0: pl.ds(1, 8), 1: pl.ds(8, 1), 3: pl.ds(1, 1)}
    y_dst = {0: pl.ds(1, 8), 1: pl.ds(0, 1), 3: pl.ds(9, 1)}
    out = []
    k = 0
    for i in (0, 1, 2):
        for j in (0, 1, 3):
            if i or j:
                out.append(
                    pltpu.make_async_remote_copy(
                        xe.at[x_src[i], y_src[j], rows],
                        xe.at[x_dst[i], y_dst[j], rows],
                        sems.at[0],
                        sems.at[1],
                        device_id=near[k],
                        device_id_type=MESH,
                    )
                )
                k += 1
    return out


def wait_bytes(ref, sem):
    pltpu.make_async_copy(ref, ref, sem).wait()


class Sum:
    def __init__(self, src, parts, tower, out, sems, place):
        self.src, self.parts, self.tower, self.out, self.sems = src, parts, tower, out, sems
        _, _, self.z, self.mine, self.plane, self.chunk, self.column, _ = place

    def send(self, src, dst, pair, dev):
        pltpu.make_async_remote_copy(
            src, dst, self.sems.at[pair], self.sems.at[pair + 1], device_id=dev, device_id_type=MESH
        ).start()

    def scatter(self):
        for k, dev in enumerate(self.plane):
            self.send(self.src.at[self.chunk[k]], self.parts.at[k], 0, dev)

    def climb(self, change=None):
        wait_bytes(self.parts, self.sems.at[1])
        total = self.src[self.mine]
        for k in range(31):
            total = total + self.parts[k]
        self.tower[self.z] = total if change is None else change(total)
        for dev in self.column.values():
            self.send(self.tower.at[self.z], self.tower.at[self.z], 2, dev)

    def spread(self):
        wait_bytes(self.tower.at[pl.ds(0, 15)], self.sems.at[3])
        total = self.tower[0]
        for k in range(1, 16):
            total = total + self.tower[k]
        self.out[self.mine] = total
        for dev in self.plane:
            self.send(self.out.at[self.mine], self.out.at[self.mine], 4, dev)

    def collect(self):
        wait_bytes(self.out.at[pl.ds(0, 31)], self.sems.at[5])

    def drain(self):
        wait_bytes(self.parts, self.sems.at[0])
        wait_bytes(self.tower.at[pl.ds(0, 15)], self.sems.at[2])
        wait_bytes(self.out.at[pl.ds(0, 31)], self.sems.at[4])


def relayout(basis, xe, wide):
    for b, rows in ((2, B2), (0, B0), (1, B1)):
        for x in range(2):
            wide[...] = basis[b, :, x].astype(F32).reshape(C * 8, 128)
            for y in range(8):
                xe[1 + x, 1 + y, rows, :] = wide[pl.ds(y, C, stride=8), :].astype(BF16)


def coefficients(cell_map, table, coef, s, ycol):
    row = lax.broadcasted_iota(jnp.int32, (8, 128), 0)
    lane = lax.broadcasted_iota(jnp.int32, (8, 128), 1)
    one = jnp.ones((8, 128), F32)
    zero = jnp.zeros((8, 128), F32)
    y_low = jnp.where((row == 0) & (ycol == 0), zero, one)
    y_high = jnp.where((row == 7) & (ycol == 3), zero, one)
    for x in range(2):
        cells = cell_map[x]
        is_class = [cells == k for k in range(8)]
        for o in range(27):
            dx, dy, dz = o // 9, o // 3 % 3, o % 3
            c = zero
            for k in range(8):
                c = jnp.where(is_class[k], table[k, o], c)
            if dx == 0 and x == 0:
                c = jnp.where(s == 0, zero, c)
            if dx == 2 and x == 1:
                c = jnp.where(s == 127, zero, c)
            if dy == 0:
                c = c * y_low
            if dy == 2:
                c = c * y_high
            if dz == 0:
                c = pltpu.roll(jnp.where(lane == 0, zero, c), 127, 1)
            if dz == 2:
                c = pltpu.roll(jnp.where(lane == 127, zero, c), 1, 1)
            coef[pl.ds(x * 8 * 32 + o, 8, stride=32), :] = c


def is_own(x, y):
    return x in (1, 2) and 1 <= y <= 8


def total_of(acc):
    return (acc[1] + pltpu.roll(acc[0], 1, 1) + pltpu.roll(acc[2], 127, 1)).astype(BF16)


def split_stencil(xe, rows, coef, held, local, put):
    for x in range(2):
        for y in range(8):
            table = coef.at[pl.ds((x * 8 + y) * 32, 32)]
            acc = [None, None, None] if local else [held[x * 8 + y, dz] for dz in range(3)]
            for dx in range(3):
                for dy in range(3):
                    if is_own(x + dx, y + dy) != local:
                        continue
                    piece = xe[x + dx, y + dy, rows, :].astype(F32)
                    for dz in range(3):
                        o = 9 * dx + 3 * dy + dz
                        term = table[o : o + 1, :] * piece
                        acc[dz] = term if acc[dz] is None else acc[dz] + term
            if local:
                for dz in range(3):
                    held[x * 8 + y, dz] = acc[dz]
            else:
                put(x, y, total_of(acc))


def stencil(xe, rows, coef, put):
    for x in range(2):

        def body(y, carry):
            table = coef.at[pl.ds(pl.multiple_of((x * 8 + y) * 32, 32), 32)]
            acc = [jnp.zeros((C, 128), F32) for _ in range(3)]
            for dx in range(3):
                for dy in range(3):
                    piece = xe[x + dx, y + dy, rows, :].astype(F32)
                    for dz in range(3):
                        o = 9 * dx + 3 * dy + dz
                        acc[dz] = acc[dz] + table[o : o + 1, :] * piece
            put(x, y, total_of(acc))
            return carry

        lax.fori_loop(0, 8, body, 0)


def own_planes(xe, rows):
    return jnp.concatenate([xe[1 + x, 1 + y, rows, :] for x in range(2) for y in range(8)], axis=1)


def gram(left, right):
    return lax.dot_general(left, right, NT, preferred_element_type=F32)


def pack(src, k, v):
    size = src.shape[1]
    for i in range(v.shape[0] // size):
        src[k + i] = v[i * size : (i + 1) * size]


def project(f_full, g):
    col = lax.broadcasted_iota(jnp.int32, (C, 256), 1)
    keep = col < 192
    first = jnp.where(keep, f_full, 0.0)
    first_b = first.astype(BF16).astype(F32)
    second = jnp.where(keep, first - fdot(first_b, g, NN), 0.0)
    second_b = second.astype(BF16).astype(F32)
    rest = jnp.where(keep, second - fdot(second_b, g, NN), 0.0)
    both = first_b + second_b
    pad = jnp.zeros((C, 256), F32)
    lane = lax.broadcasted_iota(jnp.int32, (C, 128), 1)
    own = pltpu.roll(f_full[:, 128:256], 64, 1)
    square = (
        own
        - fdot(first, jnp.concatenate([both, pad], axis=0), NT)
        - fdot(both, jnp.concatenate([rest, pad], axis=0), NT)
    )
    system = jnp.where(lane < C, square, 0.0)
    return first + second, both, rest, system


def splat(v, lane):
    return jnp.broadcast_to(v[:, lane:lane + 1], (8, 128))


def eliminate(m):
    sub = lax.broadcasted_iota(jnp.int32, (8, 128), 0)
    out = [None] * 8
    for j in range(0, 64, 4):
        t, q = j // 8, j % 8
        r = [jnp.broadcast_to(m[t][q + a : q + a + 1, :], (8, 128)) for a in range(4)]
        p = [[splat(r[a], j + b) if b >= a else None for b in range(4)] for a in range(4)]
        det = p[0][0] * p[1][1] - p[0][1] * p[0][1]
        inv = 1.0 / det
        y = [[(p[1][1] * p[0][b] - p[0][1] * p[1][b]) * inv, (p[0][0] * p[1][b] - p[0][1] * p[0][b]) * inv] for b in (2, 3)]
        s22 = p[2][2] - p[0][2] * y[0][0] - p[1][2] * y[0][1]
        s23 = p[2][3] - p[0][2] * y[1][0] - p[1][2] * y[1][1]
        s33 = p[3][3] - p[0][3] * y[1][0] - p[1][3] * y[1][1]
        det2 = s22 * s33 - s23 * s23
        r2 = r[2] - y[0][0] * r[0] - y[0][1] * r[1]
        r3 = r[3] - y[1][0] * r[0] - y[1][1] * r[1]
        if j < 60:
            inv2 = 1.0 / det2
            x0 = (p[1][1] * r[0] - p[0][1] * r[1]) * inv
            x1 = (p[0][0] * r[1] - p[0][1] * r[0]) * inv
            x2 = (s33 * r2 - s23 * r3) * inv2
            x3 = (s22 * r3 - s23 * r2) * inv2
            x0 = x0 - y[0][0] * x2 - y[1][0] * x3
            x1 = x1 - y[0][1] * x2 - y[1][1] * x3
            for v in range(t if q == 0 else t + 1, 8):
                c = [splat(m[v], j + b) for b in range(4)]
                new = m[v] - (c[0] * x0 + c[1] * x1) - (c[2] * x2 + c[3] * x3)
                m[v] = jnp.where(sub >= 4, new, m[v]) if v == t else new
        a0 = lax.rsqrt(p[0][0])
        a1 = lax.rsqrt(det * (1.0 / p[0][0]))
        a2 = lax.rsqrt(s22)
        a3 = lax.rsqrt(det2 * (1.0 / s22))
        u = [r[0] * a0, (r[1] - (p[0][1] * (1.0 / p[0][0])) * r[0]) * a1, r2 * a2, (r3 - (s23 * (1.0 / s22)) * r2) * a3]
        o = out[t] if q else u[3]
        for a in range(4):
            o = jnp.where(sub == q + a, u[a], o)
        out[t] = o
    return out


def factor(system):
    row = lax.broadcasted_iota(jnp.int32, (C, 128), 0)
    lane = lax.broadcasted_iota(jnp.int32, (C, 128), 1)
    diag = jnp.where(lane == row, system, 0.0)
    across = jnp.sum(diag, axis=1, keepdims=True)
    along = jnp.sum(diag, axis=0, keepdims=True)
    scale = lax.rsqrt(across)
    unit = lax.rsqrt(along)
    m = jnp.where(lane < C, system * scale * unit, jnp.where(lane == row + C, scale, 0.0))
    m = jnp.concatenate(eliminate([m[8 * v : 8 * v + 8] for v in range(8)]), axis=0)
    return jnp.where(lane < C, m * (along * unit), m)


def split(v):
    high = v.astype(BF16)
    return high, (v - high.astype(F32)).astype(BF16)


def mixed(weights, v):
    w = lax.dot_general(jnp.concatenate(weights, axis=0), v, NN, preferred_element_type=F32)
    return (w[0:C] + w[C : 2 * C]).astype(BF16)


def kernel(
    table_hbm, basis_hbm, map_hbm,
    w_hbm, proj_hbm, tri_hbm,
    out_w, out_proj, out_tri, table, basis, cell_map, xe, wide, coef, held, image, gm,
    src0, parts0, tower0, sum0, src1, parts1, tower1, sum1, src2, parts2, tower2, sum2,
    halo_sems, sum_sems, in_sems, out_sems, vouched,
):
    place = places()
    s, ycol, z, p, plane, chunk, column, near = place
    barrier = pltpu.get_barrier_semaphore()
    greeted = [column[d] for d in (4, 12, 3, 13, 2, 14, 1, 15)] + plane + near
    for dev in greeted:
        pl.semaphore_signal(barrier, inc=1, device_id=dev, device_id_type=MESH)
    loads = [
        pltpu.make_async_copy(basis_hbm, basis, in_sems.at[0]),
        pltpu.make_async_copy(map_hbm, cell_map, in_sems.at[1]),
        pltpu.make_async_copy(table_hbm, table, in_sems.at[2]),
    ]
    for load in loads:
        load.start()
    zero = Sum(src0, parts0, tower0, sum0, sum_sems.at[0], place)
    one = Sum(src1, parts1, tower1, sum1, sum_sems.at[1], place)
    two = Sum(src2, parts2, tower2, sum2, sum_sems.at[2], place)

    loads[0].wait()
    relayout(basis, xe, wide)
    loads[1].wait()
    loads[2].wait()
    coefficients(cell_map, table, coef, s, ycol)
    v = own_planes(xe, pl.ds(0, 192))
    g = gram(v, v[0:128])
    pack(src0, 0, g)
    g = gram(v[128:192], v[128:192])
    pack(src0, 24, jnp.concatenate([g, g], axis=1))

    split_stencil(xe, B2, coef, held, True, None)
    pl.semaphore_wait(barrier, len(greeted))
    for copy in halo_copies(xe, B2, halo_sems.at[0], near):
        copy.start()
    zero.scatter()
    for dev in (column[4], column[12]):
        pl.semaphore_signal(vouched, inc=1, device_id=dev, device_id_type=MESH)
    for copy in halo_copies(xe, B1, halo_sems.at[1], near):
        copy.start()
    moved = xe.at[pl.ds(0, 3), pl.ds(0, 8), B2]

    def put_w(x, y, v):
        xe[x + 1, y + 1, IM, :] = v
        image[x * 8 + y, C : 2 * C, :] = v

    def put_at(k):
        def put(x, y, v):
            image[x * 8 + y, k * C : (k + 1) * C, :] = v

        return put

    wait_bytes(moved, halo_sems.at[0, 1])
    split_stencil(xe, B2, coef, held, False, put_w)

    x = own_planes(xe, pl.ds(0, 256))
    f = gram(x[192:256], x)
    pack(src1, 0, f[:, 0:128])
    pack(src1, 16, f[:, 128:256])
    one.scatter()
    pl.semaphore_wait(vouched, 2)
    zero.climb()
    for k, rows in ((2, B0), (3, IM)):
        for copy in halo_copies(xe, rows, halo_sems.at[k], near):
            copy.start()
    wait_bytes(moved, halo_sems.at[1, 1])
    stencil(xe, B1, coef, put_at(0))
    one.climb()
    wait_bytes(moved, halo_sems.at[2, 1])
    stencil(xe, B0, coef, put_at(2))
    zero.spread()
    wait_bytes(moved, halo_sems.at[3, 1])
    stencil(xe, IM, coef, put_at(3))
    x = own_planes(xe, pl.ds(0, 256))
    y = jnp.concatenate([image[k] for k in range(16)], axis=1)
    for i, left in enumerate((x, y)):
        g = gram(left, y)
        for k in range(32):
            for half in range(2):
                at = 16 * i + 8 * half
                src2[k, at : at + 8, :] = g[8 * k : 8 * k + 8, 128 * half : 128 * half + 128]
    one.spread()
    two.scatter()
    zero.collect()
    scale = 1.0 / (256 * 32 * 128)
    gm[0:192, 0:128] = sum0[0:24].reshape(192, 128) * scale
    gm[0:128, 128:192] = jnp.transpose(gm[128:192, 0:128])
    gm[0:192, 192:256] = jnp.zeros((192, 64), F32)
    gm[192:256, :] = jnp.zeros((64, 256), F32)
    gm[128:192, 128:192] = sum0[24:32].reshape(64, 128)[:, 0:64] * scale
    one.collect()

    f = jnp.concatenate([sum1[0:16].reshape(64, 128), sum1[16:32].reshape(64, 128)], axis=1) * scale
    proj, both, rest, system = project(f, gm[...])
    out_proj[0] = proj

    col = lax.broadcasted_iota(jnp.int32, (C, 256), 1)
    row = lax.broadcasted_iota(jnp.int32, (C, 256), 0)
    mix = jnp.where(col == row + 192, 1.0, -both)
    empty = jnp.zeros((C, 256), F32)
    mix_both = jnp.concatenate(
        [jnp.concatenate([mix, empty], axis=1), jnp.concatenate([empty, mix], axis=1)], axis=0
    )

    def contract(total):
        wide_row = jnp.concatenate([total[8 * k : 8 * k + 8] for k in range(4)], axis=1)
        return fdot(wide_row, mix_both, NT)

    two.climb(contract)

    for k in range(4):
        wait_bytes(moved, halo_sems.at[k, 0])
    weights = split(mix)
    x = own_planes(xe, pl.ds(0, 256))
    y = jnp.concatenate([image[k] for k in range(16)], axis=1)
    for rows, v in ((B0, mixed(weights, x)), (IM, mixed(weights, y))):
        for k in range(16):
            xe[1 + k // 8, 1 + k % 8, rows, :] = v[:, 128 * k : 128 * k + 128]

    done = factor(system)
    out_tri[0] = done
    inverse = pltpu.roll(done, 64, 1)[:, 0:C].astype(BF16).astype(F32)
    none = jnp.zeros((C, C), F32)
    q_left = fdot(inverse, rest[:, 0:128], NN)
    q_own = fdot(fdot(inverse, system[:, 0:C], NN), inverse, NT)
    gm[128:192, 0:128] = q_left
    gm[0:128, 128:192] = jnp.transpose(q_left)
    gm[128:192, 128:192] = q_own
    twice = jnp.concatenate(
        [jnp.concatenate([inverse, none], axis=1), jnp.concatenate([none, inverse], axis=1)], axis=0
    )

    two.spread()
    two.collect()
    h = sum2[...].reshape(256, 128) * scale
    own = fdot(mix, h, NN)
    h = jnp.concatenate([h[0:128, 0:C], own[:, 0:C], pltpu.roll(own, 64, 1)[:, 0:C]], axis=0)
    h = fdot(inverse, h, NT)
    f = jnp.concatenate([h[:, 0:128], fdot(h[:, 128:256], twice, NT)], axis=1)
    proj, both, rest, system = project(f, gm[...])
    out_proj[1] = proj
    lane = lax.broadcasted_iota(jnp.int32, (C, 128), 1)
    unit = lax.broadcasted_iota(jnp.int32, (C, 128), 0) + C
    right = fdot(jnp.where(lane < C, -both[:, 128:256], jnp.where(lane == unit, 1.0, 0.0)), twice, NN)
    weights = split(jnp.concatenate([-both[:, 0:128], right], axis=1))
    out_w[...] = mixed(weights, own_planes(xe, pl.ds(0, 256)))
    stores = [
        pltpu.make_async_copy(out_proj, proj_hbm, out_sems.at[0]),
        pltpu.make_async_copy(out_w, w_hbm, out_sems.at[1]),
        pltpu.make_async_copy(out_tri, tri_hbm, out_sems.at[2]),
    ]
    stores[0].start()
    stores[1].start()
    out_tri[1] = factor(system)
    stores[2].start()
    zero.drain()
    one.drain()
    two.drain()
    for store in stores:
        store.wait()


def finish(w_hbm, proj_hbm, tri_hbm, out_block, out_proj, out_tri, w, proj, tri, wide, sems):
    loads = [
        pltpu.make_async_copy(tri_hbm, tri, sems.at[0]),
        pltpu.make_async_copy(w_hbm, w, sems.at[1]),
        pltpu.make_async_copy(proj_hbm, proj, sems.at[2]),
    ]
    for load in loads:
        load.start()
    for load in loads:
        load.wait()
    inverse = pltpu.roll(tri[1], 64, 1)[:, 0:C].astype(BF16)
    q = lax.dot_general(inverse, w[...], NN, preferred_element_type=F32)
    for x in range(2):
        for y in range(8):
            k = (x * 8 + y) * 128
            wide[pl.ds(y, C, stride=8), :] = q[:, k : k + 128]
        out_block[:, x] = wide[...].reshape(C, 8, 128).astype(BF16)
    row = lax.broadcasted_iota(jnp.int32, (C, C), 0)
    col = lax.broadcasted_iota(jnp.int32, (C, C), 1)
    first = proj[0]
    out_proj[0] = jnp.concatenate([first[:, 128:192], first[:, 0:128]], axis=1)
    out_proj[1] = proj[1][:, 0:192]
    for step in range(2):
        out_tri[step] = jnp.where(row >= col, jnp.transpose(tri[step])[0:C], 0.0)


def sum_scratch(sent, kept):
    return [pltpu.VMEM((count, size, 128), F32) for count, size in ((32, sent), (31, sent), (16, kept), (32, kept))]


def shards(basis, cell_map, table):
    vmem = pl.BlockSpec(memory_space=pltpu.VMEM)
    hbm = pl.BlockSpec(memory_space=pltpu.MemorySpace.HBM)
    found = pl.pallas_call(
        kernel,
        out_shape=(
            jax.ShapeDtypeStruct((C, 2048), BF16),
            jax.ShapeDtypeStruct((2, C, 256), F32),
            jax.ShapeDtypeStruct((2, C, 128), F32),
        ),
        in_specs=[hbm, hbm, hbm],
        out_specs=(hbm, hbm, hbm),
        scratch_shapes=[
            pltpu.VMEM((C, 2048), BF16),
            pltpu.VMEM((2, C, 256), F32),
            pltpu.VMEM((2, C, 128), F32),
            pltpu.SMEM((8, 27), F32),
            pltpu.VMEM((3, C, 2, 8, 128), BF16),
            pltpu.VMEM((2, 8, 128), jnp.int32),
            pltpu.VMEM((4, 10, 256, 128), BF16),
            pltpu.VMEM((C * 8, 128), F32),
            pltpu.VMEM((16 * 32, 128), F32),
            pltpu.VMEM((16, 3, C, 128), F32),
            pltpu.VMEM((16, 256, 128), BF16),
            pltpu.VMEM((256, 256), F32),
            *sum_scratch(8, 8),
            *sum_scratch(4, 4),
            *sum_scratch(32, 8),
            pltpu.SemaphoreType.DMA((4, 2)),
            pltpu.SemaphoreType.DMA((3, 6)),
            pltpu.SemaphoreType.DMA((3,)),
            pltpu.SemaphoreType.DMA((3,)),
            pltpu.SemaphoreType.REGULAR,
        ],
        compiler_params=pltpu.CompilerParams(
            collective_id=0, has_side_effects=True, vmem_limit_bytes=63 * 1024 * 1024
        ),
    )(table, basis, cell_map)
    block, proj, lower = pl.pallas_call(
        finish,
        out_shape=(
            jax.ShapeDtypeStruct((C, 2, 8, 128), BF16),
            jax.ShapeDtypeStruct((2, C, 192), F32),
            jax.ShapeDtypeStruct((2, C, C), F32),
        ),
        in_specs=[hbm, hbm, hbm],
        out_specs=(vmem, vmem, vmem),
        scratch_shapes=[
            pltpu.VMEM((C, 2048), BF16),
            pltpu.VMEM((2, C, 256), F32),
            pltpu.VMEM((2, C, 128), F32),
            pltpu.VMEM((C * 8, 128), F32),
            pltpu.SemaphoreType.DMA((3,)),
        ],
        compiler_params=pltpu.CompilerParams(vmem_limit_bytes=63 * 1024 * 1024),
    )(*found)
    return block, jnp.swapaxes(proj, 1, 2), lower


def solution(mesh):
    placed = (P(None, None, "slab", "col", None), P("slab", "col", None), P())
    return jax.shard_map(
        shards,
        mesh=mesh,
        in_specs=placed,
        out_specs=(P(None, "slab", "col", None), P(), P()),
        check_vma=False,
    )
```
